256 devices in a mesh: gx: 32 (over z, y_hi, core), gy: 8 (over y_lo, x).
Axes of the slice: x: 4, y: 4 (y_hi: 2, y_lo: 2; y = y_hi * 2 + y_lo), z: 8, core: 2. Of those that a mesh axis runs over, the one named last changes fastest.
Arguments:
- field: bfloat16 [256, 512, 256], P('gx', 'gy'), may hold values from -6 to 6
- norm_gain: float32 [2, 256], replicated, may hold values from 0.1 to 1.9
- inner_weight: bfloat16 [2, 256, 1024], replicated, may hold values from -0.375 to 0.375
- state_weight: bfloat16 [2, 256, 128], replicated, may hold values from -0.375 to 0.375
- step_weight: bfloat16 [2, 256, 8], replicated, may hold values from -0.375 to 0.375
- step_bias: float32 [2, 8], replicated, may hold values from -1 to 1
- decay_rate: float32 [2, 8], replicated, may hold values from 0.0005859375 to 0.05, as said below
- out_gain: float32 [2, 512], replicated, may hold values from 0.1 to 1.9
- out_weight: bfloat16 [2, 512, 256], replicated, may hold values from -0.25 to 0.25
Outputs:
- mixed: bfloat16 [256, 512, 256], P('gx', 'gy')
The draws below stay inside these ranges and needn't reach their ends.
Inputs may be any that keep to these rules, and one draw needn't show every extreme that they name: `decay_rate`: decay rate of each layer's heads.
All inputs are finite; a program needn't handle non-finite values.
Results may differ from the reference program's by a relative error of at most 0.024.
Values may be sent and summed in bfloat16 or wider, within the bound.
No kernel may reach another device: no remote copies, remote signals or barrier semaphores. Data moves between devices by JAX's collectives and lax.ppermute only.
A program may use at most 64 MiB of HBM per device.

```python
import math
import jax
import jax.numpy as jnp
from jax import lax

D = 256
E = 512
H = 8
P_SIZE = 64
N = 64
BLOCK = 64
NX = 256
NY = 512


def draw_decay_rate(key, part):
    key = jax.random.fold_in(key, 11)
    first, second, third = jax.random.split(key, 3)
    share = 0.5
    picked = jax.random.uniform(first, (2, H)) < share
    extent = jnp.array([NX, NY], jnp.float32)[:, None]
    slow = jnp.exp(jax.random.uniform(second, (2, H), minval=math.log(0.3), maxval=math.log(1.5))) / extent
    fast = jnp.exp(jax.random.uniform(third, (2, H), minval=math.log(1.0 / 60.0), maxval=math.log(1.0 / 20.0)))
    return jnp.where(picked, slow, fast).astype(jnp.float32)


def levels(rng, shape, cuts, smallest, high):
    def one(position, shards_of):
        steps = jax.random.uniform(jax.random.fold_in(jax.random.fold_in(rng, 6), position), (shards_of,), jnp.float32, smallest / len(cuts), high / len(cuts))
        return jnp.repeat(jnp.exp(steps), shape[position] // shards_of).reshape((-1,) + (1,) * (len(shape) - position - 1))

    level = one(*cuts[0])
    for cut in cuts[1:]:
        level = level * one(*cut)
    return level


def normal_values(own_key, shape, deviation, most, cuts=(), kind=jnp.bfloat16):
    entries = deviation * jax.random.normal(own_key, shape, jnp.float32)
    if cuts:
        entries = entries * levels(own_key, shape, cuts, -0.22, 0.18)
    return jnp.clip(entries, -most, most).astype(kind)


def setup_inputs(seed: int = 0) -> dict:
    key_list = jax.random.split(jax.random.key(seed), 10)
    return {
        "field": normal_values(key_list[0], (NX, NY, D), 1.0, 6.0, ((0, 32), (1, 8))),
        "norm_gain": jnp.clip(1.0 + 0.18 * jax.random.normal(key_list[1], (2, D), jnp.float32), 0.1, 1.9),
        "inner_weight": normal_values(key_list[2], (2, D, 2 * E), D ** -0.5, 0.375),
        "state_weight": normal_values(key_list[3], (2, D, 2 * N), D ** -0.5, 0.375),
        "step_weight": normal_values(key_list[4], (2, D, H), D ** -0.5, 0.375),
        "step_bias": jnp.clip(jax.random.uniform(key_list[5], (2, H), jnp.float32, -1.0, 1.0), -1.0, 1.0),
        "decay_rate": draw_decay_rate(jax.random.fold_in(key_list[9], 71), 0),
        "out_gain": jnp.clip(1.0 + 0.18 * jax.random.normal(key_list[7], (2, E), jnp.float32), 0.1, 1.9),
        "out_weight": normal_values(key_list[8], (2, E, D), E ** -0.5, 0.25),
    }


EPSILON = 1e-05

def normalize(block, gain):
    values = block.astype(jnp.float32)
    scale = lax.rsqrt(lax.optimization_barrier(jnp.mean(values * values, axis=-1, keepdims=True)) + EPSILON)
    return lax.optimization_barrier((values * scale * gain).astype(jnp.bfloat16))

def project(normed, layer, inner_weight, state_weight, step_weight, step_bias, decay_rate):
    length, lines, width = normed.shape
    flat = normed.reshape(length * lines, width)
    raw = jnp.dot(flat, inner_weight[layer][:, E:], preferred_element_type=jnp.float32)
    inputs = lax.optimization_barrier(jax.nn.silu(raw).astype(jnp.bfloat16)).reshape(length, lines, H, P_SIZE)
    states = lax.optimization_barrier(jnp.dot(flat, state_weight[layer], preferred_element_type=jnp.float32).astype(jnp.bfloat16))
    enter = states[:, :N].reshape(length, lines, N)
    leave = states[:, N:].reshape(length, lines, N)
    steps = jax.nn.softplus(jnp.dot(flat, step_weight[layer], preferred_element_type=jnp.float32) + step_bias[layer])
    steps = steps.reshape(length, lines, H)
    logdecay = -steps * decay_rate[layer]
    return (inputs, enter, leave, steps, logdecay)

def block_terms(inputs, enter, leave, steps, logdecay):
    span = inputs.shape[0]
    running = jnp.cumsum(logdecay, axis=0)
    scores = jnp.einsum('tmn,smn->mts', leave.astype(jnp.float32), enter.astype(jnp.float32))
    across = jnp.transpose(running, (1, 2, 0))
    gap = across[:, :, :, None] - across[:, :, None, :]
    causal = jnp.arange(span)[:, None] >= jnp.arange(span)[None, :]
    decays = jnp.where(causal, jnp.exp(jnp.where(causal, gap, 0.0)), 0.0)
    mixing = scores[:, None] * decays * jnp.transpose(steps, (1, 2, 0))[:, :, None, :]
    mixing = lax.optimization_barrier(mixing.astype(jnp.bfloat16))
    local_out = jnp.einsum('mhts,smhp->tmhp', mixing.astype(jnp.float32), inputs.astype(jnp.float32))
    tail = jnp.exp(running[-1][None] - running) * steps
    carried = lax.optimization_barrier((inputs.astype(jnp.float32) * tail[..., None]).astype(jnp.bfloat16))
    end_state = jnp.einsum('smhp,smn->mhpn', carried.astype(jnp.float32), enter.astype(jnp.float32))
    return (local_out, jnp.exp(running), jnp.exp(running[-1]), end_state)

def with_state(local_out, growth, leave, state):
    rounded = lax.optimization_barrier(state.astype(jnp.bfloat16))
    incoming = jnp.einsum('tmn,mhpn->tmhp', leave.astype(jnp.float32), rounded.astype(jnp.float32))
    return local_out + growth[..., None] * incoming

def finish(summed, gates, gain, weight):
    length, lines = (gates.shape[0], gates.shape[1])
    gated = summed.reshape(gates.shape) * jax.nn.silu(gates)
    scale = lax.rsqrt(lax.optimization_barrier(jnp.mean(gated * gated, axis=-1, keepdims=True)) + EPSILON)
    normed = (gated * scale * gain).astype(jnp.bfloat16)
    product = jnp.dot(normed.reshape(length * lines, -1), weight, preferred_element_type=jnp.float32)
    return product.reshape(length, lines, -1)

def mix_lines(stream, layer, weights):
    norm_gain, inner_weight, state_weight, step_weight, step_bias, decay_rate, out_gain, out_weight = weights
    length, lines, width = stream.shape
    count = length // BLOCK
    span = BLOCK
    blocks = stream.reshape(count, span, lines, width)

    def prepare(block):
        normed = normalize(block, norm_gain[layer])
        return project(normed, layer, inner_weight, state_weight, step_weight, step_bias, decay_rate)
    projected = lax.map(prepare, blocks)
    zero = jnp.zeros((lines, H, P_SIZE, N), jnp.float32)

    def forward(state, item):
        local_out, growth, total, end_state = block_terms(*item)
        result = with_state(local_out, growth, item[2], state)
        return (total[:, :, None, None] * state + end_state, result)
    _, ahead = lax.scan(forward, zero, projected)

    def backward(state, item):
        block, parts, front = item
        flipped = tuple((jnp.flip(part, 0) for part in parts))
        local_out, growth, total, end_state = block_terms(*flipped)
        behind = jnp.flip(with_state(local_out, growth, flipped[2], state), 0)
        normed = normalize(block, norm_gain[layer])
        gates = jnp.dot(normed.reshape(span * lines, width), inner_weight[layer][:, :E], preferred_element_type=jnp.float32)
        change = finish(front + behind, gates.reshape(span, lines, E), out_gain[layer], out_weight[layer])
        updated = (block.astype(jnp.float32) + change).astype(jnp.bfloat16)
        return (total[:, :, None, None] * state + end_state, updated)
    _, result = lax.scan(backward, zero, (blocks, projected, ahead), reverse=True)
    return result.reshape(length, lines, width)

def mix_layer(stream, layer, weights):
    length, lines, width = stream.shape
    group = math.gcd(lines, 64)
    shaped = jnp.transpose(stream.reshape(length, lines // group, group, width), (1, 0, 2, 3))
    result = lax.map(lambda piece: mix_lines(piece, layer, weights), shaped)
    return jnp.transpose(result, (1, 0, 2, 3)).reshape(length, lines, width)

def reference(field, norm_gain, inner_weight, state_weight, step_weight, step_bias, decay_rate, out_gain, out_weight):
    weights = (norm_gain, inner_weight, state_weight, step_weight, step_bias, decay_rate, out_gain, out_weight)
    stream = mix_layer(field, 0, weights)
    swapped = mix_layer(jnp.swapaxes(stream, 0, 1), 1, weights)
    return jnp.swapaxes(swapped, 0, 1)
```

```python
import functools

import jax
import jax.numpy as jnp
import numpy as np
from jax import lax
from jax.experimental import pallas as pl
from jax.experimental.pallas import tpu as pltpu
from jax.sharding import PartitionSpec as P

EPSILON = 1e-05
CHUNK = 128
HEADS = 8
SIZE = 64
ORDER = 64
INNER = HEADS * SIZE
F32 = jnp.float32
BF16 = jnp.bfloat16


def spread_matrix():
    rows = np.arange(CHUNK)
    cols = np.arange(INNER)
    blocks = []
    for q in range(5):
        blocks.append((rows[:, None] // 16 == q) & (rows[:, None] % 8 == cols[None] // SIZE))
    cols = np.arange(HEADS * 2 * ORDER)
    kind = 5 + (cols % (2 * ORDER)) // ORDER
    blocks.append(
        (rows[:, None] // 16 == kind[None]) & (rows[:, None] % 8 == cols[None] // (2 * ORDER))
    )
    return np.concatenate(blocks, 1).astype(np.float32)


def sum_matrix():
    s = np.arange(CHUNK)
    below = (s[:, None] < s[None, :]) + 0.5 * (s[:, None] == s[None, :])
    return np.concatenate([below, np.ones((CHUNK, CHUNK))], 1).astype(np.float32)


def gather_matrix():
    i = np.arange(2 * CHUNK)
    source = 2 * (i % CHUNK) + i // CHUNK
    return (source[:, None] == np.arange(2 * CHUNK)[None, :]).astype(np.float32)


def dot(a, b, dims=((1,), (0,))):
    return lax.dot_general(a, b, (dims, ((), ())), preferred_element_type=F32)


def silu(v):
    return 0.5 * v * (1.0 + jnp.tanh(0.5 * v))


def column(row):
    n = row.shape[1]
    square = lax.broadcasted_iota(jnp.int32, (n, n), 0) == lax.broadcasted_iota(
        jnp.int32, (n, n), 1
    )
    return jnp.sum(jnp.where(square, jnp.broadcast_to(row, (n, n)), 0.0), 1, keepdims=True)


def layer_kernel(
    layer,
    lines,
    interleaved,
    x_ref,
    norm_ref,
    inner_ref,
    state_ref,
    step_ref,
    bias_ref,
    rate_ref,
    gain_ref,
    out_w_ref,
    spread_ref,
    sums_ref,
    perm_ref,
    o_ref,
):
    tokens = x_ref.shape[0]
    chunks = tokens // CHUNK
    per_line = chunks // lines
    raw = x_ref[...]
    if interleaved:
        perm = perm_ref[...]
        parts = [
            dot(perm, raw[256 * a : 256 * a + 256]) for a in range(tokens // 256)
        ]
        h = jnp.concatenate(
            [p[CHUNK * l : CHUNK * l + CHUNK] for l in range(2) for p in parts], 0
        )
    else:
        h = raw.astype(F32)
    scale = lax.rsqrt(jnp.mean(h * h, axis=1, keepdims=True) + EPSILON)
    normed = (h * scale * norm_ref[layer : layer + 1, :]).astype(BF16)

    inner = inner_ref[0]
    state_w = state_ref[0]
    gates = dot(normed, inner[:, :INNER])
    inputs = silu(dot(normed, inner[:, INNER:])).astype(BF16)
    leave_w = state_w[:, ORDER:]
    leave2 = dot(normed, jnp.concatenate([leave_w, leave_w], 1)).astype(BF16)
    enter_t = dot(state_w, normed, ((0,), (1,)))[:ORDER].astype(BF16)
    raw_steps = dot(step_ref[0], normed, ((0,), (1,))) + column(bias_ref[layer : layer + 1, :])
    steps = jnp.maximum(raw_steps, 0.0) + jnp.log1p(jnp.exp(-jnp.abs(raw_steps)))
    decay = -steps * column(rate_ref[layer : layer + 1, :])
    steps = jnp.concatenate([steps[:, CHUNK * k : CHUNK * k + CHUNK] for k in range(chunks)], 0)
    decay = jnp.concatenate([decay[:, CHUNK * k : CHUNK * k + CHUNK] for k in range(chunks)], 0)
    first = decay.astype(BF16)
    rest = decay - first.astype(F32)
    second = rest.astype(BF16)
    third = (rest - second.astype(F32)).astype(BF16)
    summed = dot(jnp.concatenate([first, second, third], 0), sums_ref[...])
    n = HEADS * chunks
    summed = summed[:n] + summed[n : 2 * n] + summed[2 * n :]
    mid = summed[:, :CHUNK]
    whole = summed[:, CHUNK:]
    lead = jnp.exp(mid)
    tail = jnp.exp(whole - mid)
    entry = steps * jnp.exp(-0.5 * decay)
    growth = jnp.exp(0.5 * decay)
    total = jnp.exp(whole)
    quantities = (entry, entry * tail, entry * lead, growth, total, lead, tail)

    t_pos = lax.broadcasted_iota(jnp.int32, (CHUNK, CHUNK), 0)
    s_pos = lax.broadcasted_iota(jnp.int32, (CHUNK, CHUNK), 1)
    double = jnp.where(t_pos == s_pos, 2.0, 1.0)
    first_half = s_pos < SIZE
    spread_b = spread_ref[...]

    columns = []
    wides = []
    ends_f = []
    ends_b = []
    totals = []
    for k in range(chunks):
        rows = slice(CHUNK * k, CHUNK * k + CHUNK)
        own = slice(HEADS * k, HEADS * k + HEADS)
        pieces = []
        for q in quantities:
            upper = q[own].astype(BF16).astype(F32)
            pieces += [upper, q[own] - upper]
        pieces += [mid[own], jnp.zeros((HEADS, CHUNK), F32)]
        turned = jnp.transpose(jnp.concatenate(pieces, 0))
        columns.append(turned[:, 14 * HEADS : 15 * HEADS])
        wide = dot(turned.astype(BF16), spread_b)
        x = inputs[rows].astype(F32)
        entered = (x * wide[:, :INNER]).astype(BF16)
        carried_f = (x * wide[:, INNER : 2 * INNER]).astype(BF16)
        carried_b = (x * wide[:, 2 * INNER : 3 * INNER]).astype(BF16)
        e_t = enter_t[:, rows]
        ends_f.append(dot(e_t, carried_f))
        ends_b.append(dot(e_t, carried_b))
        totals.append(wide[0:1, 4 * INNER : 5 * INNER])
        wides.append((entered, wide[:, 3 * INNER : 4 * INNER], wide[:, 5 * INNER :]))

    states_f = [None] * chunks
    states_b = [None] * chunks
    zero = jnp.zeros((ORDER, INNER), F32)
    for line in range(lines):
        state = zero
        for k in range(line * per_line, (line + 1) * per_line):
            states_f[k] = state.astype(BF16)
            state = totals[k] * state + ends_f[k]
        state = zero
        for k in reversed(range(line * per_line, (line + 1) * per_line)):
            states_b[k] = state.astype(BF16)
            state = totals[k] * state + ends_b[k]

    results = []
    for k in range(chunks):
        rows = slice(CHUNK * k, CHUNK * k + CHUNK)
        entered, grow, sides = wides[k]
        right = jnp.concatenate([entered, states_f[k], states_b[k]], 0)
        leave = leave2[rows]
        scores = dot(leave[:, :ORDER], enter_t[:, rows]) * double
        leave = leave.astype(F32)
        mixed = []
        for pair in range(HEADS // 2):
            lefts = []
            for head in (2 * pair, 2 * pair + 1):
                gap = columns[k][:, head : head + 1] - mid[HEADS * k + head : HEADS * k + head + 1]
                mixing = (scores * jnp.exp(-jnp.abs(gap))).astype(BF16)
                side = (leave * sides[:, CHUNK * head : CHUNK * head + CHUNK]).astype(BF16)
                lefts.append(jnp.concatenate([mixing, side], 1))
            both = dot(
                jnp.concatenate(lefts, 0), right[:, CHUNK * pair : CHUNK * pair + CHUNK]
            )
            mixed.append(jnp.where(first_half, both[:CHUNK], both[CHUNK:]))
        gated = jnp.concatenate(mixed, 1) * grow * silu(gates[rows])
        scale = lax.rsqrt(jnp.mean(gated * gated, axis=1, keepdims=True) + EPSILON)
        rounded = (gated * scale * gain_ref[layer : layer + 1, :]).astype(BF16)
        results.append((h[rows] + dot(rounded, out_w_ref[0])).astype(BF16))

    if interleaved:
        perm = perm_ref[...]
        half = tokens // 256
        for a in range(half):
            o_ref[256 * a : 256 * a + 256, :] = dot(
                perm, jnp.concatenate([results[a], results[half + a]], 0), ((0,), (0,))
            ).astype(BF16)
    else:
        for k in range(chunks):
            o_ref[CHUNK * k : CHUNK * k + CHUNK, :] = results[k]


def mix(x, layer, lines, interleaved, weights):
    norm_gain, inner_weight, state_weight, step_weight, step_bias, decay_rate, out_gain, out_weight = weights
    whole = lambda a: pl.BlockSpec(a.shape, lambda i: (0,) * a.ndim)
    part = lambda a: pl.BlockSpec((1,) + a.shape[1:], lambda i: (layer, 0, 0))
    consts = (
        jnp.asarray(spread_matrix(), BF16),
        jnp.asarray(sum_matrix(), BF16),
        jnp.asarray(gather_matrix(), BF16),
    )
    return pl.pallas_call(
        functools.partial(layer_kernel, layer, lines, interleaved),
        grid=(1,),
        out_shape=jax.ShapeDtypeStruct(x.shape, BF16),
        in_specs=[
            whole(x),
            whole(norm_gain),
            part(inner_weight),
            part(state_weight),
            part(step_weight),
            whole(step_bias),
            whole(decay_rate),
            whole(out_gain),
            part(out_weight),
        ]
        + [whole(c) for c in consts],
        out_specs=whole(x),
        compiler_params=pltpu.CompilerParams(vmem_limit_bytes=40 * 1024 * 1024),
        name=f"mix_layer_{layer}",
    )(
        x,
        norm_gain,
        inner_weight,
        state_weight,
        step_weight,
        step_bias,
        decay_rate,
        out_gain,
        out_weight,
        *consts,
    )


def on_device(gx, gy, field, *weights):
    nx, ny, width = field.shape
    lines = ny // gx
    sent = jnp.swapaxes(field.reshape(nx, gx, lines, width), 0, 1).reshape(gx, nx * lines, width)
    taken = lax.all_to_all(sent, "gx", 0, 0, tiled=True).reshape(gx * nx * lines, width)
    stream = mix(taken, 0, lines, True, weights)
    taken = lax.all_to_all(
        stream.reshape(gx * nx, lines, width), ("gx", "gy"), 0, 0, tiled=True
    )
    taken = jnp.swapaxes(taken.reshape(gx, gy, lines, width), 0, 1)
    stream = mix(taken.reshape(gy * gx * lines, width), 1, 1, False, weights)
    return lax.all_to_all(stream.reshape(gy, ny, width), "gy", 0, 0, tiled=True)


def solution(mesh):
    in_specs = (P("gx", "gy", None), P(), P(), P(), P(), P(), P(), P(), P())
    return jax.shard_map(
        functools.partial(on_device, mesh.shape["gx"], mesh.shape["gy"]),
        mesh=mesh,
        in_specs=in_specs,
        out_specs=P("gx", "gy", None),
        check_vma=False,
    )
```

```python
import functools

import jax
import jax.numpy as jnp
import numpy as np
from jax import lax
from jax.experimental import pallas as pl
from jax.experimental.pallas import tpu as pltpu
from jax.sharding import PartitionSpec as P

EPSILON = 1e-05
CHUNK = 128
HEADS = 8
SIZE = 64
ORDER = 64
INNER = HEADS * SIZE
F32 = jnp.float32
BF16 = jnp.bfloat16


def spread_matrix():
    rows = np.arange(CHUNK)
    cols = np.arange(INNER)
    blocks = []
    for q in range(4):
        blocks.append((rows[:, None] // 16 == q) & (rows[:, None] % 8 == cols[None] // SIZE))
    cols = np.arange(HEADS * 2 * ORDER)
    kind = 4 + (cols % (2 * ORDER)) // ORDER
    blocks.append(
        (rows[:, None] // 16 == kind[None]) & (rows[:, None] % 8 == cols[None] // (2 * ORDER))
    )
    return np.concatenate(blocks, 1).astype(np.float32)


def positions(rows, cols):
    return (
        lax.broadcasted_iota(jnp.int32, (rows, cols), 0),
        lax.broadcasted_iota(jnp.int32, (rows, cols), 1),
    )


def sum_matrix():
    s, t = positions(CHUNK, CHUNK)
    below = jnp.where(s < t, 1.0, jnp.where(s == t, 0.5, 0.0))
    return jnp.concatenate([below, jnp.ones((CHUNK, CHUNK), F32)], 1).astype(BF16)


def gather_matrix(source):
    i, j = positions(2 * CHUNK, 2 * CHUNK)
    return jnp.where(source(i // CHUNK, i % CHUNK) == j, 1.0, 0.0).astype(BF16)


def arriving(line, x):
    return 16 * (x // 8) + 8 * line + x % 8


def leaving(line, x):
    return 2 * x + line


def dot(a, b, dims=((1,), (0,))):
    return lax.dot_general(a, b, (dims, ((), ())), preferred_element_type=F32)


def silu(v):
    return 0.5 * v * (1.0 + jnp.tanh(0.5 * v))


def column(row):
    n = row.shape[1]
    square = lax.broadcasted_iota(jnp.int32, (n, n), 0) == lax.broadcasted_iota(
        jnp.int32, (n, n), 1
    )
    return jnp.sum(jnp.where(square, jnp.broadcast_to(row, (n, n)), 0.0), 1, keepdims=True)


def layer_kernel(
    layer,
    lines,
    interleaved,
    x_ref,
    norm_ref,
    inner_ref,
    state_ref,
    step_ref,
    bias_ref,
    rate_ref,
    gain_ref,
    out_w_hbm,
    spread_ref,
    o_ref,
    out_w_ref,
    out_w_sem,
):
    out_copy = pltpu.make_async_copy(out_w_hbm.at[layer], out_w_ref, out_w_sem)
    out_copy.start()
    tokens = x_ref.shape[0]
    chunks = tokens // CHUNK
    per_line = chunks // lines
    raw = x_ref[...]
    if interleaved:
        perm = gather_matrix(arriving)
        parts = [
            dot(perm, raw[256 * a : 256 * a + 256]) for a in range(tokens // 256)
        ]
        h = jnp.concatenate(
            [p[CHUNK * l : CHUNK * l + CHUNK] for l in range(2) for p in parts], 0
        )
    else:
        h = raw.astype(F32)
    scale = lax.rsqrt(jnp.mean(h * h, axis=1, keepdims=True) + EPSILON)
    normed = (h * scale * norm_ref[layer : layer + 1, :]).astype(BF16)

    inner = inner_ref[0]
    state_w = state_ref[0]
    gates = dot(normed, inner[:, :INNER])
    inputs = silu(dot(normed, inner[:, INNER:])).astype(BF16)
    leave_w = state_w[:, ORDER:]
    leave2 = dot(normed, jnp.concatenate([leave_w, leave_w], 1)).astype(BF16)
    enter_t = dot(state_w, normed, ((0,), (1,)))[:ORDER].astype(BF16)
    raw_steps = dot(step_ref[0], normed, ((0,), (1,))) + column(bias_ref[layer : layer + 1, :])
    steps = jnp.maximum(raw_steps, 0.0) + jnp.log1p(jnp.exp(-jnp.abs(raw_steps)))
    decay = -steps * column(rate_ref[layer : layer + 1, :])
    steps = jnp.concatenate([steps[:, CHUNK * k : CHUNK * k + CHUNK] for k in range(chunks)], 0)
    decay = jnp.concatenate([decay[:, CHUNK * k : CHUNK * k + CHUNK] for k in range(chunks)], 0)
    first = decay.astype(BF16)
    rest = decay - first.astype(F32)
    second = rest.astype(BF16)
    third = (rest - second.astype(F32)).astype(BF16)
    summed = dot(jnp.concatenate([first, second, third], 0), sum_matrix())
    n = HEADS * chunks
    summed = summed[:n] + summed[n : 2 * n] + summed[2 * n :]
    mid = summed[:, :CHUNK]
    whole = summed[:, CHUNK:]
    lead = jnp.exp(mid)
    tail = jnp.exp(whole - mid)
    entry = steps * jnp.exp(-0.5 * decay)
    growth = jnp.exp(0.5 * decay)
    total = jnp.exp(whole)
    quantities = (entry, entry * tail, entry * lead, growth, lead, tail)

    t_pos, s_pos = positions(CHUNK, CHUNK)
    double = jnp.where(t_pos == s_pos, 2.0, 1.0)
    first_half = s_pos < SIZE
    spread_b = spread_ref[...]

    columns = []
    wides = []
    ends_f = []
    ends_b = []
    totals = []
    for k in range(chunks):
        rows = slice(CHUNK * k, CHUNK * k + CHUNK)
        own = slice(HEADS * k, HEADS * k + HEADS)
        pieces = []
        for q in quantities:
            upper = q[own].astype(BF16).astype(F32)
            pieces += [upper, q[own] - upper]
        pieces += [mid[own], jnp.zeros((3 * HEADS, CHUNK), F32)]
        turned = jnp.transpose(jnp.concatenate(pieces, 0))
        columns.append(turned[:, 12 * HEADS : 13 * HEADS])
        wide = dot(turned.astype(BF16), spread_b)
        x = inputs[rows].astype(F32)
        entered = (x * wide[:, :INNER]).astype(BF16)
        carried_f = (x * wide[:, INNER : 2 * INNER]).astype(BF16)
        carried_b = (x * wide[:, 2 * INNER : 3 * INNER]).astype(BF16)
        e_t = enter_t[:, rows]
        ends_f.append(dot(e_t, carried_f))
        ends_b.append(dot(e_t, carried_b))
        totals.append(
            jnp.concatenate(
                [
                    jnp.where(
                        first_half[:1],
                        total[HEADS * k + h : HEADS * k + h + 1],
                        total[HEADS * k + h + 1 : HEADS * k + h + 2],
                    )
                    for h in range(0, HEADS, 2)
                ],
                1,
            )
        )
        wides.append((entered, wide[:, 3 * INNER : 4 * INNER], wide[:, 4 * INNER :]))

    states_f = [None] * chunks
    states_b = [None] * chunks
    zero = jnp.zeros((ORDER, INNER), F32)
    for line in range(lines):
        state = zero
        for k in range(line * per_line, (line + 1) * per_line):
            states_f[k] = state.astype(BF16)
            state = totals[k] * state + ends_f[k]
        state = zero
        for k in reversed(range(line * per_line, (line + 1) * per_line)):
            states_b[k] = state.astype(BF16)
            state = totals[k] * state + ends_b[k]

    out_copy.wait()
    results = []
    for k in range(chunks):
        rows = slice(CHUNK * k, CHUNK * k + CHUNK)
        entered, grow, sides = wides[k]
        right = jnp.concatenate([entered, states_f[k], states_b[k]], 0)
        leave = leave2[rows]
        scores = dot(leave[:, :ORDER], enter_t[:, rows]) * double
        leave = leave.astype(F32)
        mixed = []
        for pair in range(HEADS // 2):
            lefts = []
            for head in (2 * pair, 2 * pair + 1):
                gap = columns[k][:, head : head + 1] - mid[HEADS * k + head : HEADS * k + head + 1]
                mixing = (scores * jnp.exp(-jnp.abs(gap))).astype(BF16)
                side = (leave * sides[:, CHUNK * head : CHUNK * head + CHUNK]).astype(BF16)
                lefts.append(jnp.concatenate([mixing, side], 1))
            both = dot(
                jnp.concatenate(lefts, 0), right[:, CHUNK * pair : CHUNK * pair + CHUNK]
            )
            mixed.append(jnp.where(first_half, both[:CHUNK], both[CHUNK:]))
        gated = jnp.concatenate(mixed, 1) * grow * silu(gates[rows])
        scale = lax.rsqrt(jnp.mean(gated * gated, axis=1, keepdims=True) + EPSILON)
        rounded = (gated * scale * gain_ref[layer : layer + 1, :]).astype(BF16)
        results.append((h[rows] + dot(rounded, out_w_ref[...])).astype(BF16))

    if interleaved:
        perm = gather_matrix(leaving)
        half = tokens // 256
        for a in range(half):
            o_ref[256 * a : 256 * a + 256, :] = dot(
                perm, jnp.concatenate([results[a], results[half + a]], 0), ((0,), (0,))
            ).astype(BF16)
    else:
        for k in range(chunks):
            o_ref[CHUNK * k : CHUNK * k + CHUNK, :] = results[k]


def mix(x, layer, lines, interleaved, weights):
    norm_gain, inner_weight, state_weight, step_weight, step_bias, decay_rate, out_gain, out_weight = weights
    whole = lambda a: pl.BlockSpec(a.shape, lambda i: (0,) * a.ndim)
    part = lambda a: pl.BlockSpec((1,) + a.shape[1:], lambda i: (layer, 0, 0))
    spread = jnp.asarray(spread_matrix(), BF16)
    return pl.pallas_call(
        functools.partial(layer_kernel, layer, lines, interleaved),
        grid=(1,),
        out_shape=jax.ShapeDtypeStruct(x.shape, BF16),
        in_specs=[
            whole(x),
            whole(norm_gain),
            part(inner_weight),
            part(state_weight),
            part(step_weight),
            whole(step_bias),
            whole(decay_rate),
            whole(out_gain),
            pl.BlockSpec(memory_space=pl.ANY),
            whole(spread),
        ],
        out_specs=whole(x),
        scratch_shapes=[pltpu.VMEM(out_weight.shape[1:], BF16), pltpu.SemaphoreType.DMA],
        compiler_params=pltpu.CompilerParams(vmem_limit_bytes=40 * 1024 * 1024),
        name=f"mix_layer_{layer}",
    )(
        x,
        norm_gain,
        inner_weight,
        state_weight,
        step_weight,
        step_bias,
        decay_rate,
        out_gain,
        out_weight,
        spread,
    )


def on_device(gx, gy, field, *weights):
    nx, ny, width = field.shape
    lines = ny // gx
    sent = jnp.swapaxes(field, 0, 1).reshape(gx, lines * nx, width)
    taken = lax.all_to_all(sent, "gx", 0, 0, tiled=True).reshape(gx * nx * lines, width)
    stream = mix(taken, 0, lines, True, weights)
    taken = lax.all_to_all(
        stream.reshape(gx * nx, lines, width), ("gx", "gy"), 0, 0, tiled=True
    )
    taken = jnp.swapaxes(taken.reshape(gx, gy, lines, width), 0, 1)
    stream = mix(taken.reshape(gy * gx * lines, width), 1, 1, False, weights)
    return lax.all_to_all(stream.reshape(gy, ny, width), "gy", 0, 0, tiled=True)


def solution(mesh):
    in_specs = (P("gx", "gy", None), P(), P(), P(), P(), P(), P(), P(), P())
    return jax.shard_map(
        functools.partial(on_device, mesh.shape["gx"], mesh.shape["gy"]),
        mesh=mesh,
        in_specs=in_specs,
        out_specs=P("gx", "gy", None),
        check_vma=False,
    )
```

```python
import functools

import jax
import jax.numpy as jnp
from jax import lax
from jax.experimental import pallas as pl
from jax.experimental.pallas import tpu as pltpu
from jax.sharding import PartitionSpec as P

EPSILON = 1e-05
LOG2E = 1.4426950408889634
CHUNK = 128
HEADS = 8
SIZE = 64
ORDER = 64
INNER = HEADS * SIZE
F32 = jnp.float32
BF16 = jnp.bfloat16


def positions(rows, cols):
    return (
        lax.broadcasted_iota(jnp.int32, (rows, cols), 0),
        lax.broadcasted_iota(jnp.int32, (rows, cols), 1),
    )


def sum_matrix():
    s, t = positions(CHUNK, CHUNK)
    below = jnp.where(s < t, 1.0, jnp.where(s == t, 0.5, 0.0))
    return jnp.concatenate([below, jnp.ones((CHUNK, CHUNK), F32)], 1).astype(BF16)


def gather_matrix(source):
    i, j = positions(2 * CHUNK, 2 * CHUNK)
    return jnp.where(source(i // CHUNK, i % CHUNK) == j, 1.0, 0.0).astype(BF16)


def arriving(line, x):
    return 16 * (x // 8) + 8 * line + x % 8


def leaving(line, x):
    return 2 * x + line


def dot(a, b, dims=((1,), (0,))):
    return lax.dot_general(a, b, (dims, ((), ())), preferred_element_type=F32)


def silu(v):
    return 0.5 * v * (1.0 + jnp.tanh(0.5 * v))


def column(row):
    n = row.shape[1]
    square = lax.broadcasted_iota(jnp.int32, (n, n), 0) == lax.broadcasted_iota(
        jnp.int32, (n, n), 1
    )
    return jnp.sum(jnp.where(square, jnp.broadcast_to(row, (n, n)), 0.0), 1, keepdims=True)


def layer_kernel(
    layer,
    lines,
    interleaved,
    x_ref,
    norm_ref,
    inner_ref,
    state_ref,
    step_ref,
    bias_ref,
    rate_ref,
    gain_ref,
    out_w_hbm,
    o_ref,
    out_w_ref,
    out_w_sem,
):
    out_copy = pltpu.make_async_copy(out_w_hbm.at[layer], out_w_ref, out_w_sem)
    out_copy.start()
    tokens = x_ref.shape[0]
    chunks = tokens // CHUNK
    per_line = chunks // lines
    raw = x_ref[...]
    if interleaved:
        perm = gather_matrix(arriving)
        parts = [
            dot(perm, raw[256 * a : 256 * a + 256]) for a in range(tokens // 256)
        ]
        h = jnp.concatenate(
            [p[CHUNK * l : CHUNK * l + CHUNK] for l in range(2) for p in parts], 0
        )
    else:
        h = raw.astype(F32)
    scale = lax.rsqrt(jnp.mean(h * h, axis=1, keepdims=True) + EPSILON)
    normed = (h * scale * norm_ref[layer : layer + 1, :]).astype(BF16)

    weights = jnp.concatenate(
        [
            jnp.transpose(jnp.concatenate([inner_ref[0], state_ref[0]], 1)),
            step_ref[0],
            jnp.zeros_like(step_ref[0]),
        ],
        0,
    )
    projected = dot(weights, normed, ((1,), (1,)))
    gates = projected[:INNER]
    inputs = silu(projected[INNER : 2 * INNER]).astype(BF16)
    base = 2 * INNER
    enter = projected[base : base + ORDER].astype(BF16)
    leave = projected[base + ORDER : base + 2 * ORDER].astype(BF16)
    raw_steps = projected[base + 2 * ORDER : base + 2 * ORDER + HEADS]
    raw_steps = raw_steps + column(bias_ref[layer : layer + 1, :])
    steps = jnp.maximum(raw_steps, 0.0) + jnp.log1p(jnp.exp(-jnp.abs(raw_steps)))
    decay = -steps * column(rate_ref[layer : layer + 1, :])
    steps = jnp.concatenate([steps[:, CHUNK * k : CHUNK * k + CHUNK] for k in range(chunks)], 0)
    decay = jnp.concatenate([decay[:, CHUNK * k : CHUNK * k + CHUNK] for k in range(chunks)], 0)
    first = decay.astype(BF16)
    rest = decay - first.astype(F32)
    second = rest.astype(BF16)
    third = (rest - second.astype(F32)).astype(BF16)
    summed = dot(jnp.concatenate([first, second, third], 0), sum_matrix())
    n = HEADS * chunks
    summed = summed[:n] + summed[n : 2 * n] + summed[2 * n :]
    mid = summed[:, :CHUNK]
    whole = summed[:, CHUNK:]
    lead = jnp.exp(mid)
    tail = jnp.exp(whole - mid)
    entry = steps * jnp.exp(-0.5 * decay)
    entry_tail = entry * tail
    entry_lead = entry * lead
    growth = jnp.exp(0.5 * decay)
    total = jnp.exp(whole)
    mid2 = mid * LOG2E
    mid2_columns = jnp.transpose(
        jnp.concatenate([mid2, jnp.zeros((CHUNK - n, CHUNK), F32)], 0)
    )

    s_pos, t_pos = positions(CHUNK, CHUNK)
    double = jnp.where(s_pos == t_pos, 2.0, 1.0)
    ahead_half = t_pos < ORDER

    def span(k):
        return slice(CHUNK * k, CHUNK * k + CHUNK)

    def by_head(values, rows, k):
        return jnp.concatenate(
            [
                values[SIZE * h : SIZE * h + SIZE] * rows[HEADS * k + h : HEADS * k + h + 1]
                for h in range(HEADS)
            ],
            0,
        )

    entered = []
    carried_ahead = []
    carried_behind = []
    for k in range(chunks):
        x = inputs[:, span(k)].astype(F32)
        entered.append(by_head(x, entry, k).astype(BF16))
        carried_ahead.append(by_head(x, entry_tail, k).astype(BF16))
        carried_behind.append(by_head(x, entry_lead, k).astype(BF16))

    empty = jnp.zeros((ORDER, CHUNK), BF16)
    joined = [None] * chunks
    for line in range(lines):
        start = line * per_line
        states = [jnp.zeros((INNER, CHUNK), F32)]
        for j in range(per_line - 1):
            f, b = start + j, start + per_line - 1 - j
            sides = jnp.concatenate(
                [
                    jnp.concatenate([enter[:, span(f)], empty], 1),
                    jnp.concatenate([empty, enter[:, span(b)]], 1),
                ],
                0,
            )
            end = dot(
                jnp.concatenate([carried_ahead[f], carried_behind[b]], 1), sides, ((1,), (1,))
            )
            factor = jnp.where(
                ahead_half[:HEADS],
                total[HEADS * f : HEADS * f + HEADS],
                total[HEADS * b : HEADS * b + HEADS],
            )
            states.append(by_head(states[-1], factor, 0) + end)
        for j in range(per_line):
            mirror = states[per_line - 1 - j]
            ahead = jnp.concatenate([ahead_half] * (INNER // CHUNK), 0)
            joined[start + j] = jnp.where(ahead, states[j], mirror).astype(BF16)

    gain = jnp.transpose(
        jnp.broadcast_to(gain_ref[layer : layer + 1, :], (CHUNK, INNER))
    )
    rounded = []
    for k in range(chunks):
        left = jnp.concatenate([entered[k], joined[k]], 1)
        leave_k = leave[:, span(k)]
        scores = dot(enter[:, span(k)], leave_k, ((0,), (0,))) * double
        leave_k = leave_k.astype(F32)
        mixed = []
        for pair in range(HEADS // 2):
            rights = []
            for row in (HEADS * k + 2 * pair, HEADS * k + 2 * pair + 1):
                gap = mid2_columns[:, row : row + 1] - mid2[row : row + 1]
                mixing = (scores * jnp.exp2(-jnp.abs(gap))).astype(BF16)
                rights.append(
                    jnp.concatenate(
                        [
                            mixing,
                            (leave_k * lead[row : row + 1]).astype(BF16),
                            (leave_k * tail[row : row + 1]).astype(BF16),
                        ],
                        0,
                    )
                )
            both = dot(left[CHUNK * pair : CHUNK * pair + CHUNK], jnp.concatenate(rights, 1))
            mixed += [both[:SIZE, :CHUNK], both[SIZE:, CHUNK:]]
        gated = by_head(jnp.concatenate(mixed, 0), growth, k) * silu(gates[:, span(k)])
        scale = lax.rsqrt(jnp.mean(gated * gated, axis=0, keepdims=True) + EPSILON)
        rounded.append((gated * scale * gain).astype(BF16))

    out_copy.wait()
    results = []
    for k in range(chunks):
        change = dot(rounded[k], out_w_ref[...], ((0,), (0,)))
        results.append((h[span(k)] + change).astype(BF16))
    if interleaved:
        perm = gather_matrix(leaving)
        half = tokens // 256
        for a in range(half):
            o_ref[256 * a : 256 * a + 256, :] = dot(
                perm, jnp.concatenate([results[a], results[half + a]], 0), ((0,), (0,))
            ).astype(BF16)
    else:
        for k in range(chunks):
            o_ref[span(k), :] = results[k]


def mix(x, layer, lines, interleaved, weights):
    norm_gain, inner_weight, state_weight, step_weight, step_bias, decay_rate, out_gain, out_weight = weights
    whole = lambda a: pl.BlockSpec(a.shape, lambda i: (0,) * a.ndim)
    part = lambda a: pl.BlockSpec((1,) + a.shape[1:], lambda i: (layer, 0, 0))
    step_weight = jnp.swapaxes(step_weight, 1, 2)
    return pl.pallas_call(
        functools.partial(layer_kernel, layer, lines, interleaved),
        grid=(1,),
        out_shape=jax.ShapeDtypeStruct(x.shape, BF16),
        in_specs=[
            whole(x),
            whole(norm_gain),
            part(inner_weight),
            part(state_weight),
            part(step_weight),
            whole(step_bias),
            whole(decay_rate),
            whole(out_gain),
            pl.BlockSpec(memory_space=pltpu.HBM),
        ],
        out_specs=whole(x),
        scratch_shapes=[pltpu.VMEM(out_weight.shape[1:], BF16), pltpu.SemaphoreType.DMA],
        compiler_params=pltpu.CompilerParams(vmem_limit_bytes=40 * 1024 * 1024),
        name=f"mix_layer_{layer}",
    )(
        x,
        norm_gain,
        inner_weight,
        state_weight,
        step_weight,
        step_bias,
        decay_rate,
        out_gain,
        out_weight,
    )


def on_device(gx, gy, field, *weights):
    nx, ny, width = field.shape
    lines = ny // gx
    sent = jnp.swapaxes(field, 0, 1).reshape(gx, lines * nx, width)
    taken = lax.all_to_all(sent, "gx", 0, 0, tiled=True).reshape(gx * nx * lines, width)
    stream = mix(taken, 0, lines, True, weights)
    taken = lax.all_to_all(
        stream.reshape(gx * nx, lines, width), ("gx", "gy"), 0, 0, tiled=True
    )
    taken = jnp.swapaxes(taken.reshape(gx, gy, lines, width), 0, 1)
    stream = mix(taken.reshape(gy * gx * lines, width), 1, 1, False, weights)
    return lax.all_to_all(stream.reshape(gy, ny, width), "gy", 0, 0, tiled=True)


def solution(mesh):
    in_specs = (P("gx", "gy", None), P(), P(), P(), P(), P(), P(), P(), P())
    return jax.shard_map(
        functools.partial(on_device, mesh.shape["gx"], mesh.shape["gy"]),
        mesh=mesh,
        in_specs=in_specs,
        out_specs=P("gx", "gy", None),
        check_vma=False,
    )
```

```python
import functools

import jax
import jax.numpy as jnp
from jax import lax
from jax.experimental import pallas as pl
from jax.experimental.pallas import tpu as pltpu
from jax.sharding import PartitionSpec as P

EPSILON = 1e-05
LOG2E = 1.4426950408889634
CHUNK = 128
HEADS = 8
SIZE = 64
ORDER = 64
INNER = HEADS * SIZE
F32 = jnp.float32
BF16 = jnp.bfloat16


def positions(rows, cols):
    return (
        lax.broadcasted_iota(jnp.int32, (rows, cols), 0),
        lax.broadcasted_iota(jnp.int32, (rows, cols), 1),
    )


def sum_matrix():
    s, t = positions(CHUNK, CHUNK)
    below = jnp.where(s < t, 1.0, jnp.where(s == t, 0.5, 0.0))
    return jnp.concatenate([below, jnp.ones((CHUNK, CHUNK), F32)], 1).astype(BF16)


def gather_matrix(source):
    i, j = positions(2 * CHUNK, 2 * CHUNK)
    return jnp.where(source(i // CHUNK, i % CHUNK) == j, 1.0, 0.0).astype(BF16)


def arriving(line, x):
    return 16 * (x // 8) + 8 * line + x % 8


def leaving(line, x):
    return 2 * x + line


def dot(a, b, dims=((1,), (0,))):
    return lax.dot_general(a, b, (dims, ((), ())), preferred_element_type=F32)


def silu(v):
    return 0.5 * v * (1.0 + jnp.tanh(0.5 * v))


def column(row):
    n = row.shape[1]
    square = lax.broadcasted_iota(jnp.int32, (n, n), 0) == lax.broadcasted_iota(
        jnp.int32, (n, n), 1
    )
    return jnp.sum(jnp.where(square, jnp.broadcast_to(row, (n, n)), 0.0), 1, keepdims=True)


def prepare_kernel(
    norm_ref,
    inner_ref,
    state_ref,
    step_ref,
    bias_ref,
    rate_ref,
    gain_ref,
    out_w_ref,
    weights_ref,
    out_ref,
    small_ref,
):
    base = 2 * INNER + 2 * ORDER
    for layer in range(2):
        weights_ref[layer, : 2 * INNER, :] = jnp.transpose(inner_ref[layer])
        weights_ref[layer, 2 * INNER : base, :] = jnp.transpose(state_ref[layer])
        weights_ref[layer, base:, :] = jnp.concatenate(
            [step_ref[layer], jnp.zeros_like(step_ref[layer])], 0
        )
        out_ref[layer] = out_w_ref[layer]
        row = slice(layer, layer + 1)
        wide = (HEADS, INNER)
        small_ref[layer, :HEADS, :] = jnp.broadcast_to(column(bias_ref[row, :]), wide)
        small_ref[layer, HEADS : 2 * HEADS, :] = jnp.broadcast_to(column(rate_ref[row, :]), wide)
        norm = norm_ref[row, :]
        small_ref[layer, 2 * HEADS :, :] = jnp.concatenate(
            [
                gain_ref[row, :],
                jnp.concatenate([norm, norm], 1),
                jnp.zeros((HEADS - 2, INNER), F32),
            ],
            0,
        )


def prepare(norm_gain, inner, state, step, bias, rate, gain, out_weight):
    step = jnp.swapaxes(step, 1, 2)
    rows = inner.shape[2] + state.shape[2] + 2 * HEADS
    return pl.pallas_call(
        prepare_kernel,
        out_shape=(
            jax.ShapeDtypeStruct((2, rows, inner.shape[1]), BF16),
            jax.ShapeDtypeStruct(out_weight.shape, BF16),
            jax.ShapeDtypeStruct((2, 3 * HEADS, INNER), F32),
        ),
        in_specs=[pl.BlockSpec(memory_space=pltpu.VMEM)] * 8,
        out_specs=[pl.BlockSpec(memory_space=pltpu.VMEM)] * 3,
        compiler_params=pltpu.CompilerParams(vmem_limit_bytes=16 * 1024 * 1024),
        cost_estimate=pl.CostEstimate(flops=0, bytes_accessed=4 * 1024 * 1024, transcendentals=0),
        name="prepare_weights",
    )(norm_gain, inner, state, step, bias, rate, gain, out_weight)


def layer_kernel(
    layer, lines, interleaved, x_ref, weights_ref, out_w_ref, small_ref, o_ref
):
    tokens = x_ref.shape[0]
    chunks = tokens // CHUNK
    per_line = chunks // lines
    raw = x_ref[...]
    if interleaved:
        perm = gather_matrix(arriving)
        parts = [
            dot(perm, raw[256 * a : 256 * a + 256]) for a in range(tokens // 256)
        ]
        h = jnp.concatenate(
            [p[CHUNK * l : CHUNK * l + CHUNK] for l in range(2) for p in parts], 0
        )
    else:
        h = raw.astype(F32)
    scale = lax.rsqrt(jnp.mean(h * h, axis=1, keepdims=True) + EPSILON)
    normed = (h * scale * small_ref[layer, 2 * HEADS + 1 : 2 * HEADS + 2, : h.shape[1]]).astype(BF16)

    projected = dot(weights_ref[layer], normed, ((1,), (1,)))
    gates = projected[:INNER]
    inputs = silu(projected[INNER : 2 * INNER]).astype(BF16)
    base = 2 * INNER
    enter = projected[base : base + ORDER].astype(BF16)
    leave = projected[base + ORDER : base + 2 * ORDER].astype(BF16)
    raw_steps = projected[base + 2 * ORDER : base + 2 * ORDER + HEADS]
    raw_steps = raw_steps + small_ref[layer, :HEADS, :]
    steps = jnp.maximum(raw_steps, 0.0) + jnp.log1p(jnp.exp(-jnp.abs(raw_steps)))
    decay = -steps * small_ref[layer, HEADS : 2 * HEADS, :]
    steps = jnp.concatenate([steps[:, CHUNK * k : CHUNK * k + CHUNK] for k in range(chunks)], 0)
    decay = jnp.concatenate([decay[:, CHUNK * k : CHUNK * k + CHUNK] for k in range(chunks)], 0)
    first = decay.astype(BF16)
    rest = decay - first.astype(F32)
    second = rest.astype(BF16)
    third = (rest - second.astype(F32)).astype(BF16)
    summed = dot(jnp.concatenate([first, second, third], 0), sum_matrix())
    n = HEADS * chunks
    summed = summed[:n] + summed[n : 2 * n] + summed[2 * n :]
    mid = summed[:, :CHUNK]
    whole = summed[:, CHUNK:]
    lead = jnp.exp(mid)
    tail = jnp.exp(whole - mid)
    entry = steps * jnp.exp(-0.5 * decay)
    entry_tail = entry * tail
    entry_lead = entry * lead
    growth = jnp.exp(0.5 * decay)
    total = jnp.exp(whole)
    mid2 = mid * LOG2E
    mid2_columns = jnp.transpose(
        jnp.concatenate([mid2, jnp.zeros((CHUNK - n, CHUNK), F32)], 0)
    )

    s_pos, t_pos = positions(CHUNK, CHUNK)
    double = jnp.where(s_pos == t_pos, 2.0, 1.0)
    ahead_half = t_pos < ORDER

    def span(k):
        return slice(CHUNK * k, CHUNK * k + CHUNK)

    def by_head(values, rows, k):
        return jnp.concatenate(
            [
                values[SIZE * h : SIZE * h + SIZE] * rows[HEADS * k + h : HEADS * k + h + 1]
                for h in range(HEADS)
            ],
            0,
        )

    entered = []
    carried_ahead = []
    carried_behind = []
    for k in range(chunks):
        x = inputs[:, span(k)].astype(F32)
        entered.append(by_head(x, entry, k).astype(BF16))
        carried_ahead.append(by_head(x, entry_tail, k).astype(BF16))
        carried_behind.append(by_head(x, entry_lead, k).astype(BF16))

    empty = jnp.zeros((ORDER, CHUNK), BF16)
    joined = [None] * chunks
    for line in range(lines):
        start = line * per_line
        states = [jnp.zeros((INNER, CHUNK), F32)]
        for j in range(per_line - 1):
            f, b = start + j, start + per_line - 1 - j
            sides = jnp.concatenate(
                [
                    jnp.concatenate([enter[:, span(f)], empty], 1),
                    jnp.concatenate([empty, enter[:, span(b)]], 1),
                ],
                0,
            )
            end = dot(
                jnp.concatenate([carried_ahead[f], carried_behind[b]], 1), sides, ((1,), (1,))
            )
            factor = jnp.where(
                ahead_half[:HEADS],
                total[HEADS * f : HEADS * f + HEADS],
                total[HEADS * b : HEADS * b + HEADS],
            )
            states.append(by_head(states[-1], factor, 0) + end)
        for j in range(per_line):
            mirror = states[per_line - 1 - j]
            ahead = jnp.concatenate([ahead_half] * (INNER // CHUNK), 0)
            joined[start + j] = jnp.where(ahead, states[j], mirror).astype(BF16)

    gain = jnp.transpose(
        jnp.broadcast_to(small_ref[layer, 2 * HEADS : 2 * HEADS + 1, :], (CHUNK, INNER))
    )
    rounded = []
    for k in range(chunks):
        left = jnp.concatenate([entered[k], joined[k]], 1)
        leave_k = leave[:, span(k)]
        scores = dot(enter[:, span(k)], leave_k, ((0,), (0,))) * double
        leave_k = leave_k.astype(F32)
        mixed = []
        for pair in range(HEADS // 2):
            rights = []
            for row in (HEADS * k + 2 * pair, HEADS * k + 2 * pair + 1):
                gap = mid2_columns[:, row : row + 1] - mid2[row : row + 1]
                mixing = (scores * jnp.exp2(-jnp.abs(gap))).astype(BF16)
                rights.append(
                    jnp.concatenate(
                        [
                            mixing,
                            (leave_k * lead[row : row + 1]).astype(BF16),
                            (leave_k * tail[row : row + 1]).astype(BF16),
                        ],
                        0,
                    )
                )
            both = dot(left[CHUNK * pair : CHUNK * pair + CHUNK], jnp.concatenate(rights, 1))
            mixed += [both[:SIZE, :CHUNK], both[SIZE:, CHUNK:]]
        gated = by_head(jnp.concatenate(mixed, 0), growth, k) * silu(gates[:, span(k)])
        scale = lax.rsqrt(jnp.mean(gated * gated, axis=0, keepdims=True) + EPSILON)
        rounded.append((gated * scale * gain).astype(BF16))

    results = []
    for k in range(chunks):
        change = dot(rounded[k], out_w_ref[layer], ((0,), (0,)))
        results.append((h[span(k)] + change).astype(BF16))
    if interleaved:
        perm = gather_matrix(leaving)
        half = tokens // 256
        for a in range(half):
            o_ref[256 * a : 256 * a + 256, :] = dot(
                perm, jnp.concatenate([results[a], results[half + a]], 0), ((0,), (0,))
            ).astype(BF16)
    else:
        for k in range(chunks):
            o_ref[span(k), :] = results[k]


def mix(x, layer, lines, interleaved, weights):
    return pl.pallas_call(
        functools.partial(layer_kernel, layer, lines, interleaved),
        out_shape=jax.ShapeDtypeStruct(x.shape, BF16),
        in_specs=[pl.BlockSpec(memory_space=pltpu.VMEM)] * 4,
        out_specs=pl.BlockSpec(memory_space=pltpu.VMEM),
        compiler_params=pltpu.CompilerParams(vmem_limit_bytes=32 * 1024 * 1024),
        name=f"mix_layer_{layer}",
    )(x, *weights)


def on_device(gx, gy, field, *weights):
    nx, ny, width = field.shape
    weights = prepare(*weights)
    lines = ny // gx
    sent = jnp.swapaxes(field, 0, 1).reshape(gx, lines * nx, width)
    taken = lax.all_to_all(sent, "gx", 0, 0, tiled=True).reshape(gx * nx * lines, width)
    stream = mix(taken, 0, lines, True, weights)
    taken = lax.all_to_all(
        stream.reshape(gx * nx, lines, width), ("gx", "gy"), 0, 0, tiled=True
    )
    taken = jnp.swapaxes(taken.reshape(gx, gy, lines, width), 0, 1)
    stream = mix(taken.reshape(gy * gx * lines, width), 1, 1, False, weights)
    return lax.all_to_all(stream.reshape(gy, ny, width), "gy", 0, 0, tiled=True)


def solution(mesh):
    in_specs = (P("gx", "gy", None), P(), P(), P(), P(), P(), P(), P(), P())
    return jax.shard_map(
        functools.partial(on_device, mesh.shape["gx"], mesh.shape["gy"]),
        mesh=mesh,
        in_specs=in_specs,
        out_specs=P("gx", "gy", None),
        check_vma=False,
    )
```

```python
import functools

import jax
import jax.numpy as jnp
from jax import lax
from jax.experimental import pallas as pl
from jax.experimental.pallas import tpu as pltpu
from jax.sharding import PartitionSpec as P

EPSILON = 1e-05
LOG2E = 1.4426950408889634
CHUNK = 128
HEADS = 8
SIZE = 64
ORDER = 64
INNER = HEADS * SIZE
F32 = jnp.float32
BF16 = jnp.bfloat16


def positions(rows, cols):
    return (
        lax.broadcasted_iota(jnp.int32, (rows, cols), 0),
        lax.broadcasted_iota(jnp.int32, (rows, cols), 1),
    )


def sum_matrix():
    s, t = positions(CHUNK, CHUNK)
    below = jnp.where(s < t, 1.0, jnp.where(s == t, 0.5, 0.0))
    return jnp.concatenate([below, jnp.ones((CHUNK, CHUNK), F32)], 1).astype(BF16)


def dot(a, b, dims=((1,), (0,))):
    return lax.dot_general(a, b, (dims, ((), ())), preferred_element_type=F32)


def silu_of_half(v):
    return v + v * jnp.tanh(v)


def rows16(row, rows):
    piece = jnp.broadcast_to(row, (16, row.shape[1])).astype(BF16)
    return jnp.concatenate([piece] * (rows // 16), 0)


def column(row):
    n = row.shape[1]
    square = lax.broadcasted_iota(jnp.int32, (n, n), 0) == lax.broadcasted_iota(
        jnp.int32, (n, n), 1
    )
    return jnp.sum(jnp.where(square, jnp.broadcast_to(row, (n, n)), 0.0), 1, keepdims=True)


def prepare_kernel(
    norm_ref,
    inner_ref,
    state_ref,
    step_ref,
    bias_ref,
    rate_ref,
    gain_ref,
    out_w_ref,
    weights_ref,
    out_ref,
    small_ref,
):
    base = 2 * INNER + 2 * ORDER
    for layer in range(2):
        weights_ref[layer, : 2 * INNER, :] = jnp.transpose(inner_ref[layer] * 0.5)
        weights_ref[layer, 2 * INNER : base, :] = jnp.transpose(state_ref[layer])
        weights_ref[layer, base:, :] = jnp.concatenate(
            [step_ref[layer], jnp.zeros_like(step_ref[layer])], 0
        )
        row = slice(layer, layer + 1)
        gain = jnp.transpose(jnp.broadcast_to(gain_ref[row, :], (CHUNK, INNER)))
        out_ref[layer] = (
            out_w_ref[layer].astype(F32) * jnp.concatenate([gain, gain], 1)
        ).astype(BF16)
        wide = (HEADS, INNER)
        small_ref[layer, :HEADS, :] = jnp.broadcast_to(column(bias_ref[row, :]), wide)
        small_ref[layer, HEADS : 2 * HEADS, :] = jnp.broadcast_to(column(rate_ref[row, :]), wide)
        norm = norm_ref[row, :]
        small_ref[layer, 2 * HEADS :, :] = jnp.broadcast_to(
            jnp.concatenate([norm, norm], 1), wide
        )


def prepare(norm_gain, inner, state, step, bias, rate, gain, out_weight):
    step = jnp.swapaxes(step, 1, 2)
    rows = inner.shape[2] + state.shape[2] + 2 * HEADS
    return pl.pallas_call(
        prepare_kernel,
        out_shape=(
            jax.ShapeDtypeStruct((2, rows, inner.shape[1]), BF16),
            jax.ShapeDtypeStruct(out_weight.shape, BF16),
            jax.ShapeDtypeStruct((2, 3 * HEADS, INNER), F32),
        ),
        in_specs=[pl.BlockSpec(memory_space=pltpu.VMEM)] * 8,
        out_specs=[pl.BlockSpec(memory_space=pltpu.VMEM)] * 3,
        compiler_params=pltpu.CompilerParams(vmem_limit_bytes=16 * 1024 * 1024),
        cost_estimate=pl.CostEstimate(flops=0, bytes_accessed=4 * 1024 * 1024, transcendentals=0),
        name="prepare_weights",
    )(norm_gain, inner, state, step, bias, rate, gain, out_weight)


def layer_kernel(
    layer, lines, interleaved, x_ref, weights_ref, out_w_ref, small_ref, o_ref, mixed_ref
):
    tokens, width = x_ref.shape
    chunks = tokens // CHUNK
    per_line = chunks // lines
    h = x_ref[...].astype(F32)
    if interleaved:
        h = jnp.concatenate(
            [
                h[8 * (lines * g + l) : 8 * (lines * g + l) + 8]
                for l in range(lines)
                for g in range(tokens // (8 * lines))
            ],
            0,
        )
    scale = lax.rsqrt(jnp.mean(h * h, axis=1, keepdims=True) + EPSILON)
    normed = (h * scale * small_ref[layer, 2 * HEADS : 2 * HEADS + 1, : h.shape[1]]).astype(BF16)

    projected = dot(weights_ref[layer], normed, ((1,), (1,)))
    gates = projected[:INNER]
    inputs = silu_of_half(projected[INNER : 2 * INNER]).astype(BF16)
    base = 2 * INNER
    enter = projected[base : base + ORDER].astype(BF16)
    leave = projected[base + ORDER : base + 2 * ORDER].astype(BF16)
    raw_steps = projected[base + 2 * ORDER : base + 2 * ORDER + HEADS]
    raw_steps = raw_steps + small_ref[layer, :HEADS, :]
    steps = jnp.maximum(raw_steps, 0.0) + jnp.log1p(jnp.exp(-jnp.abs(raw_steps)))
    decay = -steps * small_ref[layer, HEADS : 2 * HEADS, :]
    steps = jnp.concatenate([steps[:, CHUNK * k : CHUNK * k + CHUNK] for k in range(chunks)], 0)
    decay = jnp.concatenate([decay[:, CHUNK * k : CHUNK * k + CHUNK] for k in range(chunks)], 0)
    first = decay.astype(BF16)
    rest = decay - first.astype(F32)
    second = rest.astype(BF16)
    third = (rest - second.astype(F32)).astype(BF16)
    summed = dot(jnp.concatenate([first, second, third], 0), sum_matrix())
    n = HEADS * chunks
    summed = summed[:n] + summed[n : 2 * n] + summed[2 * n :]
    mid = summed[:, :CHUNK]
    whole = summed[:, CHUNK:]
    lead = jnp.exp(mid)
    tail = jnp.exp(whole - mid)
    entry = steps * jnp.exp(-0.5 * decay)
    entry_tail = entry * tail
    entry_lead = entry * lead
    growth = jnp.exp(0.5 * decay)
    total = jnp.exp(whole)
    mid2 = mid * LOG2E
    mid2_columns = jnp.transpose(
        jnp.concatenate([mid2, jnp.zeros((CHUNK - n, CHUNK), F32)], 0)
    )

    s_pos, t_pos = positions(CHUNK, CHUNK)
    double = jnp.where(s_pos == t_pos, 2.0, 1.0)
    falling = jnp.where(s_pos < t_pos, -1.0, 1.0)
    ahead_half = t_pos < ORDER

    def span(k):
        return slice(CHUNK * k, CHUNK * k + CHUNK)

    def by_head(values, rows, k):
        return jnp.concatenate(
            [
                values[SIZE * h : SIZE * h + SIZE] * rows[HEADS * k + h : HEADS * k + h + 1]
                for h in range(HEADS)
            ],
            0,
        )

    entered = []
    carried_ahead = []
    carried_behind = []
    for k in range(chunks):
        x = inputs[:, span(k)]
        for kept, factors in (
            (entered, entry),
            (carried_ahead, entry_tail),
            (carried_behind, entry_lead),
        ):
            kept.append(
                jnp.concatenate(
                    [
                        x[SIZE * h : SIZE * h + SIZE]
                        * rows16(factors[HEADS * k + h : HEADS * k + h + 1], SIZE)
                        for h in range(HEADS)
                    ],
                    0,
                )
            )

    empty = jnp.zeros((ORDER, CHUNK), BF16)
    joined = [None] * chunks
    for line in range(lines):
        start = line * per_line
        states = [jnp.zeros((INNER, CHUNK), F32)]
        for j in range(per_line - 1):
            f, b = start + j, start + per_line - 1 - j
            sides = jnp.concatenate(
                [
                    jnp.concatenate([enter[:, span(f)], empty], 1),
                    jnp.concatenate([empty, enter[:, span(b)]], 1),
                ],
                0,
            )
            end = dot(
                jnp.concatenate([carried_ahead[f], carried_behind[b]], 1), sides, ((1,), (1,))
            )
            factor = jnp.where(
                ahead_half[:HEADS],
                total[HEADS * f : HEADS * f + HEADS],
                total[HEADS * b : HEADS * b + HEADS],
            )
            states.append(by_head(states[-1], factor, 0) + end)
        for j in range(per_line):
            mirror = states[per_line - 1 - j]
            ahead = jnp.concatenate([ahead_half] * (INNER // CHUNK), 0)
            joined[start + j] = jnp.where(ahead, states[j], mirror).astype(BF16)

    rounded = []
    for k in range(chunks):
        left = jnp.concatenate([entered[k], joined[k]], 1)
        leave_k = leave[:, span(k)]
        scores = (dot(enter[:, span(k)], leave_k, ((0,), (0,))) * double).astype(BF16)
        mixed = []
        for pair in range(HEADS // 2):
            rights = []
            for row in (HEADS * k + 2 * pair, HEADS * k + 2 * pair + 1):
                gap = mid2_columns[:, row : row + 1] - mid2[row : row + 1]
                mixing = scores * jnp.exp2(gap * falling).astype(BF16)
                rights.append(
                    jnp.concatenate(
                        [
                            mixing,
                            leave_k * rows16(lead[row : row + 1], ORDER),
                            leave_k * rows16(tail[row : row + 1], ORDER),
                        ],
                        0,
                    )
                )
            both = dot(left[CHUNK * pair : CHUNK * pair + CHUNK], jnp.concatenate(rights, 1))
            mixed += [both[:SIZE, :CHUNK], both[SIZE:, CHUNK:]]
        gated = by_head(jnp.concatenate(mixed, 0), growth, k) * silu_of_half(gates[:, span(k)])
        scale = lax.rsqrt(jnp.mean(gated * gated, axis=0, keepdims=True) + EPSILON)
        rounded.append((gated * scale).astype(BF16))

    for k in range(chunks):
        result = h[span(k)] + dot(rounded[k], out_w_ref[layer], ((0,), (0,)))
        if interleaved:
            line, first_x = k // per_line, CHUNK * (k % per_line)
            for part in range(width // 128):
                first = part * tokens + lines * first_x + line
                mixed_ref[pl.ds(first, CHUNK, stride=lines), :] = result[:, span(part)]
        else:
            o_ref[span(k), :] = result.astype(BF16)
    if interleaved:
        for part in range(width // 128):
            o_ref[:, span(part)] = mixed_ref[part * tokens : (part + 1) * tokens, :].astype(BF16)


def mix(x, layer, lines, interleaved, weights):
    return pl.pallas_call(
        functools.partial(layer_kernel, layer, lines, interleaved),
        out_shape=jax.ShapeDtypeStruct(x.shape, BF16),
        in_specs=[pl.BlockSpec(memory_space=pltpu.VMEM)] * 4,
        out_specs=pl.BlockSpec(memory_space=pltpu.VMEM),
        scratch_shapes=[pltpu.VMEM((x.size // 128, 128), F32)],
        compiler_params=pltpu.CompilerParams(vmem_limit_bytes=32 * 1024 * 1024),
        name=f"mix_layer_{layer}",
    )(x, *weights)


def on_device(gx, gy, field, *weights):
    nx, ny, width = field.shape
    weights = prepare(*weights)
    lines = ny // gx
    sent = jnp.swapaxes(field, 0, 1).reshape(gx, lines * nx, width)
    taken = lax.all_to_all(sent, "gx", 0, 0, tiled=True).reshape(gx * nx * lines, width)
    stream = mix(taken, 0, lines, True, weights)
    taken = lax.all_to_all(
        stream.reshape(gx * nx, lines, width), ("gx", "gy"), 0, 0, tiled=True
    )
    taken = jnp.swapaxes(taken.reshape(gx, gy, lines, width), 0, 1)
    stream = mix(taken.reshape(gy * gx * lines, width), 1, 1, False, weights)
    return lax.all_to_all(stream.reshape(gy, ny, width), "gy", 0, 0, tiled=True)


def solution(mesh):
    in_specs = (P("gx", "gy", None), P(), P(), P(), P(), P(), P(), P(), P())
    return jax.shard_map(
        functools.partial(on_device, mesh.shape["gx"], mesh.shape["gy"]),
        mesh=mesh,
        in_specs=in_specs,
        out_specs=P("gx", "gy", None),
        check_vma=False,
    )
```

```python
import functools

import jax
import jax.numpy as jnp
from jax import lax
from jax.experimental import pallas as pl
from jax.experimental.pallas import tpu as pltpu
from jax.sharding import PartitionSpec as P

EPSILON = 1e-05
LOG2E = 1.4426950408889634
CHUNK = 128
HEADS = 8
SIZE = 64
ORDER = 64
INNER = HEADS * SIZE
F32 = jnp.float32
BF16 = jnp.bfloat16


def positions(rows, cols):
    return (
        lax.broadcasted_iota(jnp.int32, (rows, cols), 0),
        lax.broadcasted_iota(jnp.int32, (rows, cols), 1),
    )


def sum_matrix():
    s, t = positions(CHUNK, CHUNK)
    below = jnp.where(s < t, 1.0, jnp.where(s == t, 0.5, 0.0))
    return jnp.concatenate([below, jnp.ones((CHUNK, CHUNK), F32)], 1).astype(BF16)


def dot(a, b, dims=((1,), (0,))):
    return lax.dot_general(a, b, (dims, ((), ())), preferred_element_type=F32)


def silu_of_half(v):
    return v + v * jnp.tanh(v)


def rows16(row, rows):
    piece = jnp.broadcast_to(row, (16, row.shape[1])).astype(BF16)
    return jnp.concatenate([piece] * (rows // 16), 0)


def column(row):
    n = row.shape[1]
    square = lax.broadcasted_iota(jnp.int32, (n, n), 0) == lax.broadcasted_iota(
        jnp.int32, (n, n), 1
    )
    return jnp.sum(jnp.where(square, jnp.broadcast_to(row, (n, n)), 0.0), 1, keepdims=True)


def spread_kernel(field_ref, o_ref, taken, mixed, staged, in_sems, out_sems):
    nx, ny, width = field_ref.shape
    groups = in_sems.shape[0]
    size = ny // groups
    arriving = []
    for g in range(groups):
        part = pl.ds(size * g, size)
        arriving.append(
            pltpu.make_async_copy(field_ref.at[:, part, :], taken.at[:, part, :], in_sems.at[g])
        )
        arriving[-1].start()
    leaving = []
    for g in range(groups):
        arriving[g].wait()
        rows = slice(nx * size * g, nx * size * (g + 1))
        for half in range(width // 128):
            lanes = slice(128 * half, 128 * half + 128)
            first = nx * ny * half
            for x in range(nx):
                plane = taken[x, size * g : size * g + size, lanes].astype(F32)
                mixed[pl.ds(first + nx * size * g + x, size, stride=nx), :] = plane
            staged[rows, lanes] = mixed[first + rows.start : first + rows.stop, :].astype(BF16)
        part = pl.ds(nx * size * g, nx * size)
        leaving.append(pltpu.make_async_copy(staged.at[part], o_ref.at[part], out_sems.at[g]))
        leaving[-1].start()
    for copy in leaving:
        copy.wait()


def spread(field):
    nx, ny, width = field.shape
    groups = 4
    return pl.pallas_call(
        spread_kernel,
        out_shape=jax.ShapeDtypeStruct((ny * nx, width), BF16),
        in_specs=[pl.BlockSpec(memory_space=pl.ANY)],
        out_specs=pl.BlockSpec(memory_space=pl.ANY),
        scratch_shapes=[
            pltpu.VMEM(field.shape, BF16),
            pltpu.VMEM((ny * nx * width // 128, 128), F32),
            pltpu.VMEM((ny * nx, width), BF16),
            pltpu.SemaphoreType.DMA((groups,)),
            pltpu.SemaphoreType.DMA((groups,)),
        ],
        compiler_params=pltpu.CompilerParams(vmem_limit_bytes=62 * 1024 * 1024),
        name="spread_field",
    )(field)


def prepare_kernel(
    norm_ref,
    inner_ref,
    state_ref,
    step_ref,
    bias_ref,
    rate_ref,
    gain_ref,
    out_w_ref,
    weights_ref,
    out_ref,
    small_ref,
):
    base = 2 * HEADS + 2 * ORDER
    for layer in range(2):
        weights_ref[layer, : 2 * HEADS, :] = jnp.concatenate(
            [step_ref[layer], jnp.zeros_like(step_ref[layer])], 0
        )
        weights_ref[layer, 2 * HEADS : base, :] = jnp.transpose(state_ref[layer])
        inner = jnp.transpose(inner_ref[layer] * 0.5)
        weights_ref[layer, base : base + INNER, :] = inner[INNER:]
        weights_ref[layer, base + INNER :, :] = inner[:INNER]
        row = slice(layer, layer + 1)
        gain = jnp.transpose(jnp.broadcast_to(gain_ref[row, :], (CHUNK, INNER)))
        out_ref[layer] = (
            out_w_ref[layer].astype(F32) * jnp.concatenate([gain, gain], 1)
        ).astype(BF16)
        wide = (HEADS, INNER)
        small_ref[layer, :HEADS, :] = jnp.broadcast_to(column(bias_ref[row, :]), wide)
        small_ref[layer, HEADS : 2 * HEADS, :] = jnp.broadcast_to(column(rate_ref[row, :]), wide)
        norm = norm_ref[row, :]
        small_ref[layer, 2 * HEADS :, :] = jnp.broadcast_to(
            jnp.concatenate([norm, norm], 1), wide
        )


def prepare(norm_gain, inner, state, step, bias, rate, gain, out_weight):
    step = jnp.swapaxes(step, 1, 2)
    rows = inner.shape[2] + state.shape[2] + 2 * HEADS
    return pl.pallas_call(
        prepare_kernel,
        out_shape=(
            jax.ShapeDtypeStruct((2, rows, inner.shape[1]), BF16),
            jax.ShapeDtypeStruct(out_weight.shape, BF16),
            jax.ShapeDtypeStruct((2, 3 * HEADS, INNER), F32),
        ),
        in_specs=[pl.BlockSpec(memory_space=pltpu.VMEM)] * 8,
        out_specs=[pl.BlockSpec(memory_space=pltpu.VMEM)] * 3,
        compiler_params=pltpu.CompilerParams(vmem_limit_bytes=16 * 1024 * 1024),
        cost_estimate=pl.CostEstimate(flops=0, bytes_accessed=4 * 1024 * 1024, transcendentals=0),
        name="prepare_weights",
    )(norm_gain, inner, state, step, bias, rate, gain, out_weight)


def layer_kernel(
    layer, lines, grid, x_ref, weights_ref, out_w_ref, small_ref, o_ref, mixed_ref, sorted_ref
):
    interleaved = lines > 1
    tokens, width = x_ref.shape
    chunks = tokens // CHUNK
    per_line = chunks // lines
    h = x_ref[...].astype(F32)
    if not interleaved:
        gx, gy = grid
        pair = tokens // (gx * gy)
        for part in range(width // 128):
            first = part * tokens
            mixed_ref[first : first + tokens, :] = h[:, 128 * part : 128 * part + 128]
            for b in range(gy):
                for l in range(pair):
                    source = pl.ds(first + b * pair + l, gx, stride=gy * pair)
                    target = pl.ds(first + b * gx * pair + l, gx, stride=pair)
                    sorted_ref[target, :] = mixed_ref[source, :]
        h = jnp.concatenate(
            [sorted_ref[part * tokens : part * tokens + tokens, :] for part in range(width // 128)],
            1,
        )
    else:
        h = jnp.concatenate(
            [
                h[8 * (lines * g + l) : 8 * (lines * g + l) + 8]
                for l in range(lines)
                for g in range(tokens // (8 * lines))
            ],
            0,
        )
    scale = lax.rsqrt(jnp.mean(h * h, axis=1, keepdims=True) + EPSILON)
    normed = (h * scale * small_ref[layer, 2 * HEADS : 2 * HEADS + 1, : h.shape[1]]).astype(BF16)

    projected = dot(weights_ref[layer], normed, ((1,), (1,)))
    raw_steps = projected[:HEADS]
    base = 2 * HEADS
    enter = projected[base : base + ORDER].astype(BF16)
    leave = projected[base + ORDER : base + 2 * ORDER].astype(BF16)
    base += 2 * ORDER
    inputs = silu_of_half(projected[base : base + INNER]).astype(BF16)
    gates = projected[base + INNER :]
    raw_steps = raw_steps + small_ref[layer, :HEADS, :]
    steps = jnp.maximum(raw_steps, 0.0) + jnp.log1p(jnp.exp(-jnp.abs(raw_steps)))
    decay = -steps * small_ref[layer, HEADS : 2 * HEADS, :]
    steps = jnp.concatenate([steps[:, CHUNK * k : CHUNK * k + CHUNK] for k in range(chunks)], 0)
    decay = jnp.concatenate([decay[:, CHUNK * k : CHUNK * k + CHUNK] for k in range(chunks)], 0)
    first = decay.astype(BF16)
    rest = decay - first.astype(F32)
    second = rest.astype(BF16)
    third = (rest - second.astype(F32)).astype(BF16)
    summed = dot(jnp.concatenate([first, second, third], 0), sum_matrix())
    n = HEADS * chunks
    summed = summed[:n] + summed[n : 2 * n] + summed[2 * n :]
    mid = summed[:, :CHUNK]
    whole = summed[:, CHUNK:]
    lead = jnp.exp(mid)
    tail = jnp.exp(whole - mid)
    entry = steps * jnp.exp(-0.5 * decay)
    entry_tail = entry * tail
    entry_lead = entry * lead
    growth = jnp.exp(0.5 * decay)
    total = jnp.exp(whole)
    mid2 = mid * LOG2E
    mid2_columns = jnp.transpose(
        jnp.concatenate([mid2, jnp.zeros((CHUNK - n, CHUNK), F32)], 0)
    )

    s_pos, t_pos = positions(CHUNK, CHUNK)
    double = jnp.where(s_pos == t_pos, 2.0, 1.0)
    falling = jnp.where(s_pos < t_pos, -1.0, 1.0)
    ahead_half = t_pos < ORDER

    def span(k):
        return slice(CHUNK * k, CHUNK * k + CHUNK)

    def by_head(values, rows, k):
        return jnp.concatenate(
            [
                values[SIZE * h : SIZE * h + SIZE] * rows[HEADS * k + h : HEADS * k + h + 1]
                for h in range(HEADS)
            ],
            0,
        )

    entered = []
    carried_ahead = []
    carried_behind = []
    for k in range(chunks):
        x = inputs[:, span(k)]
        for kept, factors in (
            (entered, entry),
            (carried_ahead, entry_tail),
            (carried_behind, entry_lead),
        ):
            kept.append(
                jnp.concatenate(
                    [
                        x[SIZE * h : SIZE * h + SIZE]
                        * rows16(factors[HEADS * k + h : HEADS * k + h + 1], SIZE)
                        for h in range(HEADS)
                    ],
                    0,
                )
            )

    empty = jnp.zeros((ORDER, CHUNK), BF16)
    joined = [None] * chunks
    for line in range(lines):
        start = line * per_line
        states = [jnp.zeros((INNER, CHUNK), F32)]
        for j in range(per_line - 1):
            f, b = start + j, start + per_line - 1 - j
            sides = jnp.concatenate(
                [
                    jnp.concatenate([enter[:, span(f)], empty], 1),
                    jnp.concatenate([empty, enter[:, span(b)]], 1),
                ],
                0,
            )
            end = dot(
                jnp.concatenate([carried_ahead[f], carried_behind[b]], 1), sides, ((1,), (1,))
            )
            factor = jnp.where(
                ahead_half[:HEADS],
                total[HEADS * f : HEADS * f + HEADS],
                total[HEADS * b : HEADS * b + HEADS],
            )
            states.append(by_head(states[-1], factor, 0) + end)
        for j in range(per_line):
            mirror = states[per_line - 1 - j]
            ahead = jnp.concatenate([ahead_half] * (INNER // CHUNK), 0)
            joined[start + j] = jnp.where(ahead, states[j], mirror).astype(BF16)

    rounded = []
    for k in range(chunks):
        left = jnp.concatenate([entered[k], joined[k]], 1)
        leave_k = leave[:, span(k)]
        scores = (dot(enter[:, span(k)], leave_k, ((0,), (0,))) * double).astype(BF16)
        mixed = []
        for pair in range(HEADS // 2):
            rights = []
            for row in (HEADS * k + 2 * pair, HEADS * k + 2 * pair + 1):
                gap = mid2_columns[:, row : row + 1] - mid2[row : row + 1]
                mixing = scores * jnp.exp2(gap * falling).astype(BF16)
                rights.append(
                    jnp.concatenate(
                        [
                            mixing,
                            leave_k * rows16(lead[row : row + 1], ORDER),
                            leave_k * rows16(tail[row : row + 1], ORDER),
                        ],
                        0,
                    )
                )
            both = dot(left[CHUNK * pair : CHUNK * pair + CHUNK], jnp.concatenate(rights, 1))
            mixed += [both[:SIZE, :CHUNK], both[SIZE:, CHUNK:]]
        gated = by_head(jnp.concatenate(mixed, 0), growth, k) * silu_of_half(gates[:, span(k)])
        scale = lax.rsqrt(jnp.mean(gated * gated, axis=0, keepdims=True) + EPSILON)
        rounded.append((gated * scale).astype(BF16))

    for k in range(chunks):
        result = h[span(k)] + dot(rounded[k], out_w_ref[layer], ((0,), (0,)))
        if interleaved:
            line, first_x = k // per_line, CHUNK * (k % per_line)
            for part in range(width // 128):
                first = part * tokens + lines * first_x + line
                mixed_ref[pl.ds(first, CHUNK, stride=lines), :] = result[:, span(part)]
        else:
            o_ref[span(k), :] = result.astype(BF16)
    if interleaved:
        for part in range(width // 128):
            o_ref[:, span(part)] = mixed_ref[part * tokens : (part + 1) * tokens, :].astype(BF16)


def mix(x, layer, lines, grid, weights):
    return pl.pallas_call(
        functools.partial(layer_kernel, layer, lines, grid),
        out_shape=jax.ShapeDtypeStruct(x.shape, BF16),
        in_specs=[pl.BlockSpec(memory_space=pltpu.VMEM)] * 4,
        out_specs=pl.BlockSpec(memory_space=pltpu.VMEM),
        scratch_shapes=[pltpu.VMEM((x.size // 128, 128), F32)] * 2,
        compiler_params=pltpu.CompilerParams(vmem_limit_bytes=32 * 1024 * 1024),
        name=f"mix_layer_{layer}",
    )(x, *weights)


def on_device(gx, gy, field, *weights):
    nx, ny, width = field.shape
    lines = ny // gx
    tokens = nx * ny
    weights = prepare(*weights)
    sent = spread(field).reshape(gx, lines * nx, width)
    taken = lax.all_to_all(sent, "gx", 0, 0, tiled=True).reshape(tokens, width)
    stream = mix(taken, 0, lines, (gx, gy), weights)
    taken = lax.all_to_all(
        stream.reshape(gx * nx, lines, width), ("gx", "gy"), 0, 0, tiled=True
    )
    stream = mix(taken.reshape(tokens, width), 1, 1, (gx, gy), weights)
    return lax.all_to_all(stream.reshape(gy, ny, width), "gy", 0, 0, tiled=True)


def solution(mesh):
    in_specs = (P("gx", "gy", None), P(), P(), P(), P(), P(), P(), P(), P())
    return jax.shard_map(
        functools.partial(on_device, mesh.shape["gx"], mesh.shape["gy"]),
        mesh=mesh,
        in_specs=in_specs,
        out_specs=P("gx", "gy", None),
        check_vma=False,
    )
```

```python
import functools

import jax
import jax.numpy as jnp
from jax import lax
from jax.experimental import pallas as pl
from jax.experimental.pallas import tpu as pltpu
from jax.sharding import PartitionSpec as P

EPSILON = 1e-05
LOG2E = 1.4426950408889634
CHUNK = 128
HEADS = 8
SIZE = 64
ORDER = 64
INNER = HEADS * SIZE
F32 = jnp.float32
BF16 = jnp.bfloat16


def positions(rows, cols):
    return (
        lax.broadcasted_iota(jnp.int32, (rows, cols), 0),
        lax.broadcasted_iota(jnp.int32, (rows, cols), 1),
    )


def sum_matrix():
    s, t = positions(CHUNK, CHUNK)
    below = jnp.where(s < t, 1.0, jnp.where(s == t, 0.5, 0.0))
    return jnp.concatenate([below, jnp.ones((CHUNK, CHUNK), F32)], 1).astype(BF16)


def dot(a, b, dims=((1,), (0,))):
    return lax.dot_general(a, b, (dims, ((), ())), preferred_element_type=F32)


def silu_of_half(v):
    return v + v * jnp.tanh(v)


def rows16(row, rows):
    piece = jnp.broadcast_to(row, (16, row.shape[1])).astype(BF16)
    return jnp.concatenate([piece] * (rows // 16), 0)


def column(row):
    n = row.shape[1]
    square = lax.broadcasted_iota(jnp.int32, (n, n), 0) == lax.broadcasted_iota(
        jnp.int32, (n, n), 1
    )
    return jnp.sum(jnp.where(square, jnp.broadcast_to(row, (n, n)), 0.0), 1, keepdims=True)


def spread_kernel(field_ref, o_ref, taken, mixed, staged, in_sems, out_sems):
    nx, ny, width = field_ref.shape
    groups = in_sems.shape[0]
    size = ny // groups
    arriving = []
    for g in range(groups):
        part = pl.ds(size * g, size)
        arriving.append(
            pltpu.make_async_copy(field_ref.at[:, part, :], taken.at[:, part, :], in_sems.at[g])
        )
        arriving[-1].start()
    leaving = []
    for g in range(groups):
        arriving[g].wait()
        rows = slice(nx * size * g, nx * size * (g + 1))
        for half in range(width // 128):
            lanes = slice(128 * half, 128 * half + 128)
            first = nx * ny * half
            for x in range(nx):
                plane = taken[x, size * g : size * g + size, lanes].astype(F32)
                mixed[pl.ds(first + nx * size * g + x, size, stride=nx), :] = plane
            staged[rows, lanes] = mixed[first + rows.start : first + rows.stop, :].astype(BF16)
        part = pl.ds(nx * size * g, nx * size)
        leaving.append(pltpu.make_async_copy(staged.at[part], o_ref.at[part], out_sems.at[g]))
        leaving[-1].start()
    for copy in leaving:
        copy.wait()


def spread(field):
    nx, ny, width = field.shape
    groups = 4
    return pl.pallas_call(
        spread_kernel,
        out_shape=jax.ShapeDtypeStruct((ny * nx, width), BF16),
        in_specs=[pl.BlockSpec(memory_space=pl.ANY)],
        out_specs=pl.BlockSpec(memory_space=pl.ANY),
        scratch_shapes=[
            pltpu.VMEM(field.shape, BF16),
            pltpu.VMEM((ny * nx * width // 128, 128), F32),
            pltpu.VMEM((ny * nx, width), BF16),
            pltpu.SemaphoreType.DMA((groups,)),
            pltpu.SemaphoreType.DMA((groups,)),
        ],
        compiler_params=pltpu.CompilerParams(vmem_limit_bytes=62 * 1024 * 1024),
        name="spread_field",
    )(field)


def prepare_kernel(
    norm_ref,
    inner_ref,
    state_ref,
    step_ref,
    bias_ref,
    rate_ref,
    gain_ref,
    out_w_ref,
    weights_ref,
    out_ref,
    small_ref,
):
    base = 2 * HEADS + 2 * ORDER
    for layer in range(2):
        weights_ref[layer, : 2 * HEADS, :] = jnp.concatenate(
            [step_ref[layer], jnp.zeros_like(step_ref[layer])], 0
        )
        weights_ref[layer, 2 * HEADS : base, :] = jnp.transpose(state_ref[layer])
        inner = jnp.transpose(inner_ref[layer] * 0.5)
        weights_ref[layer, base : base + INNER, :] = inner[INNER:]
        weights_ref[layer, base + INNER :, :] = inner[:INNER]
        row = slice(layer, layer + 1)
        gain = jnp.transpose(jnp.broadcast_to(gain_ref[row, :], (CHUNK, INNER)))
        out_ref[layer] = (
            out_w_ref[layer].astype(F32) * jnp.concatenate([gain, gain], 1)
        ).astype(BF16)
        wide = (HEADS, INNER)
        small_ref[layer, :HEADS, :] = jnp.broadcast_to(column(bias_ref[row, :]), wide)
        small_ref[layer, HEADS : 2 * HEADS, :] = jnp.broadcast_to(column(rate_ref[row, :]), wide)
        norm = norm_ref[row, :]
        small_ref[layer, 2 * HEADS :, :] = jnp.broadcast_to(
            jnp.concatenate([norm, norm], 1), wide
        )


def prepare(norm_gain, inner, state, step, bias, rate, gain, out_weight):
    step = jnp.swapaxes(step, 1, 2)
    rows = inner.shape[2] + state.shape[2] + 2 * HEADS
    return pl.pallas_call(
        prepare_kernel,
        out_shape=(
            jax.ShapeDtypeStruct((2, rows, inner.shape[1]), BF16),
            jax.ShapeDtypeStruct(out_weight.shape, BF16),
            jax.ShapeDtypeStruct((2, 3 * HEADS, INNER), F32),
        ),
        in_specs=[pl.BlockSpec(memory_space=pltpu.VMEM)] * 8,
        out_specs=[pl.BlockSpec(memory_space=pltpu.VMEM)] * 3,
        compiler_params=pltpu.CompilerParams(vmem_limit_bytes=16 * 1024 * 1024),
        cost_estimate=pl.CostEstimate(flops=0, bytes_accessed=4 * 1024 * 1024, transcendentals=0),
        name="prepare_weights",
    )(norm_gain, inner, state, step, bias, rate, gain, out_weight)


def layer_kernel(
    layer, lines, grid, x_ref, weights_ref, out_w_ref, small_ref, o_ref, mixed_ref, sorted_ref
):
    interleaved = lines > 1
    width = weights_ref.shape[2]
    parts = width // 128
    tokens = x_ref.size // width
    chunks = tokens // CHUNK
    per_line = chunks // lines
    h = x_ref[...].astype(F32)
    if not interleaved:
        gx, gy = grid
        pair = tokens // (gx * gy)
        mixed_ref[...] = h
        for part in range(parts):
            for l in range(pair):
                found = mixed_ref[pl.ds(l * parts + part, gx * gy, stride=pair * parts), :]
                found = jnp.swapaxes(found.reshape(gx, gy, 128), 0, 1).reshape(gx * gy, 128)
                sorted_ref[pl.ds(part * tokens + l, gx * gy, stride=pair), :] = found
        h = jnp.concatenate(
            [sorted_ref[part * tokens : part * tokens + tokens, :] for part in range(parts)], 1
        )
    else:
        h = jnp.concatenate(
            [
                h[8 * (lines * g + l) : 8 * (lines * g + l) + 8]
                for l in range(lines)
                for g in range(tokens // (8 * lines))
            ],
            0,
        )
    scale = lax.rsqrt(jnp.mean(h * h, axis=1, keepdims=True) + EPSILON)
    normed = (h * scale * small_ref[layer, 2 * HEADS : 2 * HEADS + 1, : h.shape[1]]).astype(BF16)

    rows = weights_ref.shape[1] - INNER
    projected = dot(weights_ref[layer, :rows, :], normed, ((1,), (1,)))
    raw_steps = projected[:HEADS]
    base = 2 * HEADS
    enter = projected[base : base + ORDER].astype(BF16)
    leave = projected[base + ORDER : base + 2 * ORDER].astype(BF16)
    base += 2 * ORDER
    inputs = silu_of_half(projected[base : base + INNER]).astype(BF16)
    raw_steps = raw_steps + small_ref[layer, :HEADS, :]
    steps = jnp.maximum(raw_steps, 0.0) + jnp.log1p(jnp.exp(-jnp.abs(raw_steps)))
    decay = -steps * small_ref[layer, HEADS : 2 * HEADS, :]
    steps = jnp.concatenate([steps[:, CHUNK * k : CHUNK * k + CHUNK] for k in range(chunks)], 0)
    decay = jnp.concatenate([decay[:, CHUNK * k : CHUNK * k + CHUNK] for k in range(chunks)], 0)
    first = decay.astype(BF16)
    rest = decay - first.astype(F32)
    second = rest.astype(BF16)
    third = (rest - second.astype(F32)).astype(BF16)
    summed = dot(jnp.concatenate([first, second, third], 0), sum_matrix())
    gates = dot(weights_ref[layer, rows:, :], normed, ((1,), (1,)))
    n = HEADS * chunks
    summed = summed[:n] + summed[n : 2 * n] + summed[2 * n :]
    mid = summed[:, :CHUNK]
    whole = summed[:, CHUNK:]
    lead = jnp.exp(mid)
    tail = jnp.exp(whole - mid)
    entry = steps * jnp.exp(-0.5 * decay)
    entry_tail = entry * tail
    entry_lead = entry * lead
    growth = jnp.exp(0.5 * decay)
    total = jnp.exp(whole)
    mid2 = mid * LOG2E
    mid2_columns = jnp.transpose(
        jnp.concatenate([mid2, jnp.zeros((CHUNK - n, CHUNK), F32)], 0)
    )

    s_pos, t_pos = positions(CHUNK, CHUNK)
    double = jnp.where(s_pos == t_pos, 2.0, 1.0)
    falling = jnp.where(s_pos < t_pos, -1.0, 1.0)
    ahead_half = t_pos < ORDER

    def span(k):
        return slice(CHUNK * k, CHUNK * k + CHUNK)

    def by_head(values, rows, k):
        return jnp.concatenate(
            [
                values[SIZE * h : SIZE * h + SIZE] * rows[HEADS * k + h : HEADS * k + h + 1]
                for h in range(HEADS)
            ],
            0,
        )

    entered = []
    carried_ahead = []
    carried_behind = []
    for k in range(chunks):
        x = inputs[:, span(k)]
        for kept, factors in (
            (entered, entry),
            (carried_ahead, entry_tail),
            (carried_behind, entry_lead),
        ):
            kept.append(
                jnp.concatenate(
                    [
                        x[SIZE * h : SIZE * h + SIZE]
                        * rows16(factors[HEADS * k + h : HEADS * k + h + 1], SIZE)
                        for h in range(HEADS)
                    ],
                    0,
                )
            )

    empty = jnp.zeros((ORDER, CHUNK), BF16)
    joined = [None] * chunks
    for line in range(lines):
        start = line * per_line
        states = [jnp.zeros((INNER, CHUNK), F32)]
        for j in range(per_line - 1):
            f, b = start + j, start + per_line - 1 - j
            sides = jnp.concatenate(
                [
                    jnp.concatenate([enter[:, span(f)], empty], 1),
                    jnp.concatenate([empty, enter[:, span(b)]], 1),
                ],
                0,
            )
            end = dot(
                jnp.concatenate([carried_ahead[f], carried_behind[b]], 1), sides, ((1,), (1,))
            )
            factor = jnp.where(
                ahead_half[:HEADS],
                total[HEADS * f : HEADS * f + HEADS],
                total[HEADS * b : HEADS * b + HEADS],
            )
            states.append(by_head(states[-1], factor, 0) + end)
        for j in range(per_line):
            mirror = states[per_line - 1 - j]
            ahead = jnp.concatenate([ahead_half] * (INNER // CHUNK), 0)
            joined[start + j] = jnp.where(ahead, states[j], mirror).astype(BF16)

    rounded = []
    for k in range(chunks):
        left = jnp.concatenate([entered[k], joined[k]], 1)
        leave_k = leave[:, span(k)]
        scores = (dot(enter[:, span(k)], leave_k, ((0,), (0,))) * double).astype(BF16)
        mixed = []
        for pair in range(HEADS // 2):
            rights = []
            for row in (HEADS * k + 2 * pair, HEADS * k + 2 * pair + 1):
                gap = mid2_columns[:, row : row + 1] - mid2[row : row + 1]
                mixing = scores * jnp.exp2(gap * falling).astype(BF16)
                rights.append(
                    jnp.concatenate(
                        [
                            mixing,
                            leave_k * rows16(lead[row : row + 1], ORDER),
                            leave_k * rows16(tail[row : row + 1], ORDER),
                        ],
                        0,
                    )
                )
            both = dot(left[CHUNK * pair : CHUNK * pair + CHUNK], jnp.concatenate(rights, 1))
            mixed += [both[:SIZE, :CHUNK], both[SIZE:, CHUNK:]]
        gated = by_head(jnp.concatenate(mixed, 0), growth, k) * silu_of_half(gates[:, span(k)])
        scale = lax.rsqrt(jnp.mean(gated * gated, axis=0, keepdims=True) + EPSILON)
        rounded.append((gated * scale).astype(BF16))

    for k in range(chunks):
        result = h[span(k)] + dot(rounded[k], out_w_ref[layer], ((0,), (0,)))
        if interleaved:
            line, first_x = k // per_line, CHUNK * (k % per_line)
            for part in range(parts):
                target = pl.ds((lines * first_x + line) * parts + part, CHUNK, stride=lines * parts)
                mixed_ref[target, :] = result[:, span(part)]
        else:
            o_ref[span(k), :] = result.astype(BF16)
    if interleaved:
        o_ref[...] = mixed_ref[...].astype(BF16)


def mix(x, layer, lines, grid, shape, weights):
    return pl.pallas_call(
        functools.partial(layer_kernel, layer, lines, grid),
        out_shape=jax.ShapeDtypeStruct(shape, BF16),
        in_specs=[pl.BlockSpec(memory_space=pltpu.VMEM)] * 4,
        out_specs=pl.BlockSpec(memory_space=pltpu.VMEM),
        scratch_shapes=[pltpu.VMEM((x.size // 128, 128), F32)] * 2,
        compiler_params=pltpu.CompilerParams(vmem_limit_bytes=32 * 1024 * 1024),
        name=f"mix_layer_{layer}",
    )(x, *weights)


def on_device(gx, gy, field, *weights):
    nx, ny, width = field.shape
    lines = ny // gx
    tokens = nx * ny
    weights = prepare(*weights)
    sent = spread(field).reshape(gx, lines * nx, width)
    taken = lax.all_to_all(sent, "gx", 0, 0, tiled=True).reshape(tokens, width)
    stream = mix(taken, 0, lines, (gx, gy), (2 * tokens, width // 2), weights)
    taken = lax.all_to_all(
        stream.reshape(gx * nx, -1, width // 2), ("gx", "gy"), 0, 0, tiled=True
    )
    stream = mix(taken.reshape(stream.shape), 1, 1, (gx, gy), (tokens, width), weights)
    return lax.all_to_all(stream.reshape(gy, ny, width), "gy", 0, 0, tiled=True)


def solution(mesh):
    in_specs = (P("gx", "gy", None), P(), P(), P(), P(), P(), P(), P(), P())
    return jax.shard_map(
        functools.partial(on_device, mesh.shape["gx"], mesh.shape["gy"]),
        mesh=mesh,
        in_specs=in_specs,
        out_specs=P("gx", "gy", None),
        check_vma=False,
    )
```

```python
import functools

import jax
import jax.numpy as jnp
from jax import lax
from jax.experimental import pallas as pl
from jax.experimental.pallas import tpu as pltpu
from jax.sharding import PartitionSpec as P

EPSILON = 1e-05
LOG2E = 1.4426950408889634
CHUNK = 128
HEADS = 8
SIZE = 64
ORDER = 64
INNER = HEADS * SIZE
F32 = jnp.float32
BF16 = jnp.bfloat16


def positions(rows, cols):
    return (
        lax.broadcasted_iota(jnp.int32, (rows, cols), 0),
        lax.broadcasted_iota(jnp.int32, (rows, cols), 1),
    )


def sum_matrix():
    s, t = positions(CHUNK, CHUNK)
    below = jnp.where(s < t, 1.0, jnp.where(s == t, 0.5, 0.0))
    return jnp.concatenate([below, jnp.ones((CHUNK, CHUNK), F32)], 1).astype(BF16)


def dot(a, b, dims=((1,), (0,))):
    return lax.dot_general(a, b, (dims, ((), ())), preferred_element_type=F32)


def silu_of_half(v):
    return v + v * jnp.tanh(v)


def backwards(v):
    return jnp.concatenate([v[i : i + 1] for i in reversed(range(v.shape[0]))], 0)


def rows16(row, rows):
    piece = jnp.broadcast_to(row, (16, row.shape[1])).astype(BF16)
    return jnp.concatenate([piece] * (rows // 16), 0)


def column(row):
    n = row.shape[1]
    square = lax.broadcasted_iota(jnp.int32, (n, n), 0) == lax.broadcasted_iota(
        jnp.int32, (n, n), 1
    )
    return jnp.sum(jnp.where(square, jnp.broadcast_to(row, (n, n)), 0.0), 1, keepdims=True)


def spread_kernel(field_ref, o_ref, taken, mixed, staged, in_sems, out_sems):
    nx, ny, width = field_ref.shape
    groups = in_sems.shape[0]
    size = ny // groups
    arriving = []
    for g in range(groups):
        part = pl.ds(size * g, size)
        arriving.append(
            pltpu.make_async_copy(field_ref.at[:, part, :], taken.at[:, part, :], in_sems.at[g])
        )
        arriving[-1].start()
    leaving = []
    for g in range(groups):
        arriving[g].wait()
        rows = slice(nx * size * g, nx * size * (g + 1))
        for half in range(width // 128):
            lanes = slice(128 * half, 128 * half + 128)
            first = nx * ny * half
            for x in range(nx):
                plane = taken[x, size * g : size * g + size, lanes].astype(F32)
                mixed[pl.ds(first + nx * size * g + x, size, stride=nx), :] = plane
            staged[rows, lanes] = mixed[first + rows.start : first + rows.stop, :].astype(BF16)
        part = pl.ds(nx * size * g, nx * size)
        leaving.append(pltpu.make_async_copy(staged.at[part], o_ref.at[part], out_sems.at[g]))
        leaving[-1].start()
    for copy in leaving:
        copy.wait()


def spread(field):
    nx, ny, width = field.shape
    groups = 4
    return pl.pallas_call(
        spread_kernel,
        out_shape=jax.ShapeDtypeStruct((ny * nx, width), BF16),
        in_specs=[pl.BlockSpec(memory_space=pl.ANY)],
        out_specs=pl.BlockSpec(memory_space=pl.ANY),
        scratch_shapes=[
            pltpu.VMEM(field.shape, BF16),
            pltpu.VMEM((ny * nx * width // 128, 128), F32),
            pltpu.VMEM((ny * nx, width), BF16),
            pltpu.SemaphoreType.DMA((groups,)),
            pltpu.SemaphoreType.DMA((groups,)),
        ],
        compiler_params=pltpu.CompilerParams(vmem_limit_bytes=62 * 1024 * 1024),
        name="spread_field",
    )(field)


def prepare_kernel(
    norm_ref,
    inner_ref,
    state_ref,
    step_ref,
    bias_ref,
    rate_ref,
    gain_ref,
    out_w_ref,
    weights_ref,
    out_ref,
    small_ref,
):
    base = 2 * HEADS + 2 * ORDER
    for layer in range(2):
        weights_ref[layer, : 2 * HEADS, :] = jnp.concatenate(
            [step_ref[layer], jnp.zeros_like(step_ref[layer])], 0
        )
        weights_ref[layer, 2 * HEADS : base, :] = jnp.transpose(state_ref[layer])
        inner = jnp.transpose(inner_ref[layer] * 0.5)
        weights_ref[layer, base : base + INNER, :] = inner[INNER:]
        weights_ref[layer, base + INNER :, :] = inner[:INNER]
        row = slice(layer, layer + 1)
        gain = jnp.transpose(jnp.broadcast_to(gain_ref[row, :], (CHUNK, INNER)))
        out_ref[layer] = (
            out_w_ref[layer].astype(F32) * jnp.concatenate([gain, gain], 1)
        ).astype(BF16)
        wide = (HEADS, INNER)
        small_ref[layer, :HEADS, :] = jnp.broadcast_to(column(bias_ref[row, :]), wide)
        small_ref[layer, HEADS : 2 * HEADS, :] = jnp.broadcast_to(column(rate_ref[row, :]), wide)
        norm = norm_ref[row, :]
        small_ref[layer, 2 * HEADS :, :] = jnp.broadcast_to(
            jnp.concatenate([norm, norm], 1), wide
        )


def prepare(norm_gain, inner, state, step, bias, rate, gain, out_weight):
    step = jnp.swapaxes(step, 1, 2)
    rows = inner.shape[2] + state.shape[2] + 2 * HEADS
    return pl.pallas_call(
        prepare_kernel,
        out_shape=(
            jax.ShapeDtypeStruct((2, rows, inner.shape[1]), BF16),
            jax.ShapeDtypeStruct(out_weight.shape, BF16),
            jax.ShapeDtypeStruct((2, 3 * HEADS, INNER), F32),
        ),
        in_specs=[pl.BlockSpec(memory_space=pltpu.VMEM)] * 8,
        out_specs=[pl.BlockSpec(memory_space=pltpu.VMEM)] * 3,
        compiler_params=pltpu.CompilerParams(vmem_limit_bytes=16 * 1024 * 1024),
        cost_estimate=pl.CostEstimate(flops=0, bytes_accessed=4 * 1024 * 1024, transcendentals=0),
        name="prepare_weights",
    )(norm_gain, inner, state, step, bias, rate, gain, out_weight)


def layer_kernel(
    layer, lines, grid, x_ref, weights_ref, out_w_ref, small_ref, o_ref, mixed_ref, sorted_ref
):
    interleaved = lines > 1
    width = weights_ref.shape[2]
    parts = width // 128
    tokens = x_ref.size // width
    chunks = tokens // CHUNK
    per_line = chunks // lines
    h = x_ref[...].astype(F32)
    if not interleaved:
        gx, gy = grid
        pair = tokens // (gx * gy)
        mixed_ref[...] = h
        for part in range(parts):
            for l in range(pair):
                found = mixed_ref[pl.ds(l * parts + part, gx * gy, stride=pair * parts), :]
                found = backwards(found.reshape(gx, gy, 128))
                found = backwards(jnp.swapaxes(found, 0, 1)).reshape(gx * gy, 128)
                sorted_ref[pl.ds(part * tokens + l, gx * gy, stride=pair), :] = found
        h = jnp.concatenate(
            [sorted_ref[part * tokens : part * tokens + tokens, :] for part in range(parts)], 1
        )
    else:
        h = jnp.concatenate(
            [
                h[8 * (lines * g + l) : 8 * (lines * g + l) + 8]
                for l in range(lines)
                for g in reversed(range(tokens // (8 * lines)))
            ],
            0,
        )
    scale = lax.rsqrt(jnp.mean(h * h, axis=1, keepdims=True) + EPSILON)
    normed = (h * scale * small_ref[layer, 2 * HEADS : 2 * HEADS + 1, : h.shape[1]]).astype(BF16)

    rows = weights_ref.shape[1] - INNER
    projected = dot(weights_ref[layer, :rows, :], normed, ((1,), (1,)))
    raw_steps = projected[:HEADS]
    base = 2 * HEADS
    enter = projected[base : base + ORDER].astype(BF16)
    leave = projected[base + ORDER : base + 2 * ORDER].astype(BF16)
    base += 2 * ORDER
    inputs = silu_of_half(projected[base : base + INNER]).astype(BF16)
    raw_steps = raw_steps + small_ref[layer, :HEADS, :]
    steps = jnp.maximum(raw_steps, 0.0) + jnp.log1p(jnp.exp(-jnp.abs(raw_steps)))
    decay = -steps * small_ref[layer, HEADS : 2 * HEADS, :]
    steps = jnp.concatenate([steps[:, CHUNK * k : CHUNK * k + CHUNK] for k in range(chunks)], 0)
    decay = jnp.concatenate([decay[:, CHUNK * k : CHUNK * k + CHUNK] for k in range(chunks)], 0)
    first = decay.astype(BF16)
    rest = decay - first.astype(F32)
    second = rest.astype(BF16)
    third = (rest - second.astype(F32)).astype(BF16)
    summed = dot(jnp.concatenate([first, second, third], 0), sum_matrix())
    gates = dot(weights_ref[layer, rows:, :], normed, ((1,), (1,)))
    n = HEADS * chunks
    summed = summed[:n] + summed[n : 2 * n] + summed[2 * n :]
    mid = summed[:, :CHUNK]
    whole = summed[:, CHUNK:]
    lead = jnp.exp(mid)
    tail = jnp.exp(whole - mid)
    entry = steps * jnp.exp(-0.5 * decay)
    entry_tail = entry * tail
    entry_lead = entry * lead
    growth = jnp.exp(0.5 * decay)
    total = jnp.exp(whole)
    mid2 = mid * LOG2E
    mid2_columns = jnp.transpose(
        jnp.concatenate([mid2, jnp.zeros((CHUNK - n, CHUNK), F32)], 0)
    )

    s_pos, t_pos = positions(CHUNK, CHUNK)
    double = jnp.where(s_pos == t_pos, 2.0, 1.0)
    falling = jnp.where(s_pos < t_pos, -1.0, 1.0)
    ahead_half = t_pos < ORDER

    def span(k):
        return slice(CHUNK * k, CHUNK * k + CHUNK)

    def by_head(values, rows, k):
        return jnp.concatenate(
            [
                values[SIZE * h : SIZE * h + SIZE] * rows[HEADS * k + h : HEADS * k + h + 1]
                for h in range(HEADS)
            ],
            0,
        )

    entered = []
    carried_ahead = []
    carried_behind = []
    for k in range(chunks):
        x = inputs[:, span(k)]
        for kept, factors in (
            (entered, entry),
            (carried_ahead, entry_tail),
            (carried_behind, entry_lead),
        ):
            kept.append(
                jnp.concatenate(
                    [
                        x[SIZE * h : SIZE * h + SIZE]
                        * rows16(factors[HEADS * k + h : HEADS * k + h + 1], SIZE)
                        for h in range(HEADS)
                    ],
                    0,
                )
            )

    empty = jnp.zeros((ORDER, CHUNK), BF16)
    joined = [None] * chunks
    for line in range(lines):
        start = line * per_line
        states = [jnp.zeros((INNER, CHUNK), F32)]
        for j in range(per_line - 1):
            f, b = start + j, start + per_line - 1 - j
            sides = jnp.concatenate(
                [
                    jnp.concatenate([enter[:, span(f)], empty], 1),
                    jnp.concatenate([empty, enter[:, span(b)]], 1),
                ],
                0,
            )
            end = dot(
                jnp.concatenate([carried_ahead[f], carried_behind[b]], 1), sides, ((1,), (1,))
            )
            factor = jnp.where(
                ahead_half[:HEADS],
                total[HEADS * f : HEADS * f + HEADS],
                total[HEADS * b : HEADS * b + HEADS],
            )
            states.append(by_head(states[-1], factor, 0) + end)
        for j in range(per_line):
            mirror = states[per_line - 1 - j]
            ahead = jnp.concatenate([ahead_half] * (INNER // CHUNK), 0)
            joined[start + j] = jnp.where(ahead, states[j], mirror).astype(BF16)

    rounded = []
    scales = []
    for k in range(chunks):
        left = jnp.concatenate([entered[k], joined[k]], 1)
        leave_k = leave[:, span(k)]
        scores = (dot(enter[:, span(k)], leave_k, ((0,), (0,))) * double).astype(BF16)
        mixed = []
        for pair in range(HEADS // 2):
            rights = []
            for row in (HEADS * k + 2 * pair, HEADS * k + 2 * pair + 1):
                gap = mid2_columns[:, row : row + 1] - mid2[row : row + 1]
                mixing = scores * jnp.exp2(gap * falling).astype(BF16)
                rights.append(
                    jnp.concatenate(
                        [
                            mixing,
                            leave_k * rows16(lead[row : row + 1], ORDER),
                            leave_k * rows16(tail[row : row + 1], ORDER),
                        ],
                        0,
                    )
                )
            both = dot(left[CHUNK * pair : CHUNK * pair + CHUNK], jnp.concatenate(rights, 1))
            mixed += [both[:SIZE, :CHUNK], both[SIZE:, CHUNK:]]
        gated = by_head(jnp.concatenate(mixed, 0), growth, k) * silu_of_half(gates[:, span(k)])
        rounded.append(gated.astype(BF16))
        scale = lax.rsqrt(jnp.mean(gated * gated, axis=0, keepdims=True) + EPSILON)
        scales.append(jnp.transpose(jnp.broadcast_to(scale, (CHUNK, CHUNK))))

    for k in range(chunks):
        change = dot(rounded[k], out_w_ref[layer], ((0,), (0,)))
        result = h[span(k)] + change * jnp.concatenate([scales[k]] * parts, 1)
        if interleaved:
            line, first_x = k // per_line, CHUNK * (k % per_line)
            for part in range(parts):
                target = pl.ds((lines * first_x + line) * parts + part, CHUNK, stride=lines * parts)
                mixed_ref[target, :] = result[:, span(part)]
        else:
            result = result.astype(BF16)
            size = tokens // gy
            for b in range(CHUNK // size):
                first = tokens - size * (k * (CHUNK // size) + b + 1)
                o_ref[first : first + size, :] = result[size * b : size * b + size]
    if interleaved:
        o_ref[...] = mixed_ref[...].astype(BF16)


def mix(x, layer, lines, grid, shape, weights):
    return pl.pallas_call(
        functools.partial(layer_kernel, layer, lines, grid),
        out_shape=jax.ShapeDtypeStruct(shape, BF16),
        in_specs=[pl.BlockSpec(memory_space=pltpu.VMEM)] * 4,
        out_specs=pl.BlockSpec(memory_space=pltpu.VMEM),
        scratch_shapes=[pltpu.VMEM((x.size // 128, 128), F32)] * 2,
        compiler_params=pltpu.CompilerParams(vmem_limit_bytes=32 * 1024 * 1024),
        name=f"mix_layer_{layer}",
    )(x, *weights)


def on_device(gx, gy, field, *weights):
    nx, ny, width = field.shape
    lines = ny // gx
    tokens = nx * ny
    weights = prepare(*weights)
    falling_x = [list(reversed(range(gx)))]
    falling_y = [list(reversed(range(gy)))]
    sent = spread(field).reshape(gx, lines * nx, width)
    taken = lax.all_to_all(sent, "gx", 0, 0, tiled=True, axis_index_groups=falling_x)
    taken = taken.reshape(tokens, width)
    stream = mix(taken, 0, lines, (gx, gy), (2 * tokens, width // 2), weights)
    owners = [[gy * (x // gy) + gy - 1 - x % gy for x in range(gx * nx)]]
    taken = lax.all_to_all(
        stream.reshape(gx * nx, -1, width // 2),
        ("gx", "gy"),
        0,
        0,
        tiled=True,
        axis_index_groups=owners,
    )
    stream = mix(taken.reshape(stream.shape), 1, 1, (gx, gy), (tokens, width), weights)
    return lax.all_to_all(
        stream.reshape(gy, ny, width), "gy", 0, 0, tiled=True, axis_index_groups=falling_y
    )


def solution(mesh):
    in_specs = (P("gx", "gy", None), P(), P(), P(), P(), P(), P(), P(), P())
    return jax.shard_map(
        functools.partial(on_device, mesh.shape["gx"], mesh.shape["gy"]),
        mesh=mesh,
        in_specs=in_specs,
        out_specs=P("gx", "gy", None),
        check_vma=False,
    )
```

```python
import functools

import jax
import jax.numpy as jnp
from jax import lax
from jax.experimental import pallas as pl
from jax.experimental.pallas import tpu as pltpu
from jax.sharding import PartitionSpec as P

EPSILON = 1e-05
LOG2E = 1.4426950408889634
CHUNK = 128
HEADS = 8
SIZE = 64
ORDER = 64
INNER = HEADS * SIZE
F32 = jnp.float32
BF16 = jnp.bfloat16


def positions(rows, cols):
    return (
        lax.broadcasted_iota(jnp.int32, (rows, cols), 0),
        lax.broadcasted_iota(jnp.int32, (rows, cols), 1),
    )


def sum_matrix():
    s, t = positions(CHUNK, CHUNK)
    below = jnp.where(s < t, 1.0, jnp.where(s == t, 0.5, 0.0))
    return jnp.concatenate([below, jnp.ones((CHUNK, CHUNK), F32)], 1).astype(BF16)


def dot(a, b, dims=((1,), (0,))):
    return lax.dot_general(a, b, (dims, ((), ())), preferred_element_type=F32)


def silu_of_half(v):
    return v + v * jnp.tanh(v)


def backwards(v):
    return jnp.concatenate([v[i : i + 1] for i in reversed(range(v.shape[0]))], 0)


def rows16(row, rows):
    piece = jnp.broadcast_to(row, (16, row.shape[1])).astype(BF16)
    return jnp.concatenate([piece] * (rows // 16), 0)


def column(row):
    n = row.shape[1]
    square = lax.broadcasted_iota(jnp.int32, (n, n), 0) == lax.broadcasted_iota(
        jnp.int32, (n, n), 1
    )
    return jnp.sum(jnp.where(square, jnp.broadcast_to(row, (n, n)), 0.0), 1, keepdims=True)


def spread_kernel(field_ref, o_ref, taken, mixed, staged, in_sems, out_sems):
    nx, ny, width = field_ref.shape
    groups = in_sems.shape[0]
    size = ny // groups
    arriving = []
    for g in range(groups):
        part = pl.ds(size * g, size)
        arriving.append(
            pltpu.make_async_copy(field_ref.at[:, part, :], taken.at[:, part, :], in_sems.at[g])
        )
        arriving[-1].start()
    leaving = []
    for g in range(groups):
        arriving[g].wait()
        rows = slice(nx * size * g, nx * size * (g + 1))
        for half in range(width // 128):
            lanes = slice(128 * half, 128 * half + 128)
            first = nx * ny * half
            for x in range(nx):
                plane = taken[x, size * g : size * g + size, lanes].astype(F32)
                mixed[pl.ds(first + nx * size * g + x, size, stride=nx), :] = plane
            staged[rows, lanes] = mixed[first + rows.start : first + rows.stop, :].astype(BF16)
        part = pl.ds(nx * size * g, nx * size)
        leaving.append(pltpu.make_async_copy(staged.at[part], o_ref.at[part], out_sems.at[g]))
        leaving[-1].start()
    for copy in leaving:
        copy.wait()


def spread(field):
    nx, ny, width = field.shape
    groups = 4
    return pl.pallas_call(
        spread_kernel,
        out_shape=jax.ShapeDtypeStruct((ny * nx, width), BF16),
        in_specs=[pl.BlockSpec(memory_space=pl.ANY)],
        out_specs=pl.BlockSpec(memory_space=pl.ANY),
        scratch_shapes=[
            pltpu.VMEM(field.shape, BF16),
            pltpu.VMEM((ny * nx * width // 128, 128), F32),
            pltpu.VMEM((ny * nx, width), BF16),
            pltpu.SemaphoreType.DMA((groups,)),
            pltpu.SemaphoreType.DMA((groups,)),
        ],
        compiler_params=pltpu.CompilerParams(vmem_limit_bytes=62 * 1024 * 1024),
        name="spread_field",
    )(field)


def prepare_kernel(
    norm_ref,
    inner_ref,
    state_ref,
    step_ref,
    bias_ref,
    rate_ref,
    gain_ref,
    out_w_ref,
    weights_ref,
    out_ref,
    small_ref,
):
    base = 2 * HEADS + 2 * ORDER
    for layer in range(2):
        weights_ref[layer, : 2 * HEADS, :] = jnp.concatenate(
            [step_ref[layer], jnp.zeros_like(step_ref[layer])], 0
        )
        weights_ref[layer, 2 * HEADS : base, :] = jnp.transpose(state_ref[layer])
        inner = jnp.transpose(inner_ref[layer] * 0.5)
        weights_ref[layer, base : base + INNER, :] = inner[INNER:]
        weights_ref[layer, base + INNER :, :] = inner[:INNER]
        row = slice(layer, layer + 1)
        gain = jnp.transpose(jnp.broadcast_to(gain_ref[row, :], (CHUNK, INNER)))
        out_ref[layer] = (
            out_w_ref[layer].astype(F32) * jnp.concatenate([gain, gain], 1)
        ).astype(BF16)
        wide = (HEADS, INNER)
        small_ref[layer, :HEADS, :] = jnp.broadcast_to(column(bias_ref[row, :]), wide)
        small_ref[layer, HEADS : 2 * HEADS, :] = jnp.broadcast_to(column(rate_ref[row, :]), wide)
        norm = norm_ref[row, :]
        small_ref[layer, 2 * HEADS :, :] = jnp.broadcast_to(
            jnp.concatenate([norm, norm], 1), wide
        )


def prepare(norm_gain, inner, state, step, bias, rate, gain, out_weight):
    step = jnp.swapaxes(step, 1, 2)
    rows = inner.shape[2] + state.shape[2] + 2 * HEADS
    return pl.pallas_call(
        prepare_kernel,
        out_shape=(
            jax.ShapeDtypeStruct((2, rows, inner.shape[1]), BF16),
            jax.ShapeDtypeStruct(out_weight.shape, BF16),
            jax.ShapeDtypeStruct((2, 3 * HEADS, INNER), F32),
        ),
        in_specs=[pl.BlockSpec(memory_space=pltpu.VMEM)] * 8,
        out_specs=[pl.BlockSpec(memory_space=pltpu.VMEM)] * 3,
        compiler_params=pltpu.CompilerParams(vmem_limit_bytes=16 * 1024 * 1024),
        cost_estimate=pl.CostEstimate(flops=0, bytes_accessed=4 * 1024 * 1024, transcendentals=0),
        name="prepare_weights",
    )(norm_gain, inner, state, step, bias, rate, gain, out_weight)


def layer_kernel(
    layer, lines, grid, x_ref, weights_ref, out_w_ref, small_ref, o_ref, mixed_ref, sorted_ref
):
    interleaved = lines > 1
    width = weights_ref.shape[2]
    parts = width // 128
    tokens = x_ref.size // width
    chunks = tokens // CHUNK
    per_line = chunks // lines
    gx, gy = grid
    h = x_ref[...].astype(F32)
    if not interleaved:
        pair = tokens // (gx * gy)
        mixed_ref[...] = h
        for part in range(parts):
            for l in range(pair):
                found = mixed_ref[pl.ds(l * parts + part, gx * gy, stride=pair * parts), :]
                found = jnp.swapaxes(found.reshape(gx, gy, 128), 0, 1)
                found = backwards(found).reshape(gx * gy, 128)
                sorted_ref[pl.ds(part * tokens + l, gx * gy, stride=pair), :] = found
        h = jnp.concatenate(
            [sorted_ref[part * tokens : part * tokens + tokens, :] for part in range(parts)], 1
        )
    else:
        h = jnp.concatenate(
            [
                h[8 * (lines * g + l) : 8 * (lines * g + l) + 8]
                for l in range(lines)
                for g in reversed(range(tokens // (8 * lines)))
            ],
            0,
        )
    scale = lax.rsqrt(jnp.mean(h * h, axis=1, keepdims=True) + EPSILON)
    normed = (h * scale * small_ref[layer, 2 * HEADS : 2 * HEADS + 1, : h.shape[1]]).astype(BF16)

    rows = weights_ref.shape[1] - INNER
    projected = dot(weights_ref[layer, :rows, :], normed, ((1,), (1,)))
    raw_steps = projected[:HEADS]
    base = 2 * HEADS
    enter = projected[base : base + ORDER].astype(BF16)
    leave = projected[base + ORDER : base + 2 * ORDER].astype(BF16)
    base += 2 * ORDER
    inputs = silu_of_half(projected[base : base + INNER]).astype(BF16)
    raw_steps = raw_steps + small_ref[layer, :HEADS, :]
    steps = jnp.maximum(raw_steps, 0.0) + jnp.log1p(jnp.exp(-jnp.abs(raw_steps)))
    decay = -steps * small_ref[layer, HEADS : 2 * HEADS, :]
    steps = jnp.concatenate([steps[:, CHUNK * k : CHUNK * k + CHUNK] for k in range(chunks)], 0)
    decay = jnp.concatenate([decay[:, CHUNK * k : CHUNK * k + CHUNK] for k in range(chunks)], 0)
    first = decay.astype(BF16)
    rest = decay - first.astype(F32)
    second = rest.astype(BF16)
    third = (rest - second.astype(F32)).astype(BF16)
    summed = dot(jnp.concatenate([first, second, third], 0), sum_matrix())
    gates = dot(weights_ref[layer, rows:, :], normed, ((1,), (1,)))
    n = HEADS * chunks
    summed = summed[:n] + summed[n : 2 * n] + summed[2 * n :]
    mid = summed[:, :CHUNK]
    whole = summed[:, CHUNK:]
    lead = jnp.exp(mid)
    tail = jnp.exp(whole - mid)
    entry = steps * jnp.exp(-0.5 * decay)
    entry_tail = entry * tail
    entry_lead = entry * lead
    growth = jnp.exp(0.5 * decay)
    total = jnp.exp(whole)
    mid2 = mid * LOG2E
    mid2_columns = jnp.transpose(
        jnp.concatenate([mid2, jnp.zeros((CHUNK - n, CHUNK), F32)], 0)
    )

    s_pos, t_pos = positions(CHUNK, CHUNK)
    double = jnp.where(s_pos == t_pos, 2.0, 1.0)
    falling = jnp.where(s_pos < t_pos, -1.0, 1.0)
    ahead_half = t_pos < ORDER

    def span(k):
        return slice(CHUNK * k, CHUNK * k + CHUNK)

    def by_head(values, rows, k):
        return jnp.concatenate(
            [
                values[SIZE * h : SIZE * h + SIZE] * rows[HEADS * k + h : HEADS * k + h + 1]
                for h in range(HEADS)
            ],
            0,
        )

    entered = []
    carried_ahead = []
    carried_behind = []
    for k in range(chunks):
        x = inputs[:, span(k)]
        for kept, factors in (
            (entered, entry),
            (carried_ahead, entry_tail),
            (carried_behind, entry_lead),
        ):
            kept.append(
                jnp.concatenate(
                    [
                        x[SIZE * h : SIZE * h + SIZE]
                        * rows16(factors[HEADS * k + h : HEADS * k + h + 1], SIZE)
                        for h in range(HEADS)
                    ],
                    0,
                )
            )

    empty = jnp.zeros((ORDER, CHUNK), BF16)
    joined = [None] * chunks
    for line in range(lines):
        start = line * per_line
        states = [jnp.zeros((INNER, CHUNK), F32)]
        for j in range(per_line - 1):
            f, b = start + j, start + per_line - 1 - j
            sides = jnp.concatenate(
                [
                    jnp.concatenate([enter[:, span(f)], empty], 1),
                    jnp.concatenate([empty, enter[:, span(b)]], 1),
                ],
                0,
            )
            end = dot(
                jnp.concatenate([carried_ahead[f], carried_behind[b]], 1), sides, ((1,), (1,))
            )
            factor = jnp.where(
                ahead_half[:HEADS],
                total[HEADS * f : HEADS * f + HEADS],
                total[HEADS * b : HEADS * b + HEADS],
            )
            states.append(by_head(states[-1], factor, 0) + end)
        for j in range(per_line):
            mirror = states[per_line - 1 - j]
            ahead = jnp.concatenate([ahead_half] * (INNER // CHUNK), 0)
            joined[start + j] = jnp.where(ahead, states[j], mirror).astype(BF16)

    rounded = []
    scales = []
    for k in range(chunks):
        left = jnp.concatenate([entered[k], joined[k]], 1)
        leave_k = leave[:, span(k)]
        scores = (dot(enter[:, span(k)], leave_k, ((0,), (0,))) * double).astype(BF16)
        mixed = []
        for pair in range(HEADS // 2):
            rights = []
            for row in (HEADS * k + 2 * pair, HEADS * k + 2 * pair + 1):
                gap = mid2_columns[:, row : row + 1] - mid2[row : row + 1]
                mixing = scores * jnp.exp2(gap * falling).astype(BF16)
                rights.append(
                    jnp.concatenate(
                        [
                            mixing,
                            leave_k * rows16(lead[row : row + 1], ORDER),
                            leave_k * rows16(tail[row : row + 1], ORDER),
                        ],
                        0,
                    )
                )
            both = dot(left[CHUNK * pair : CHUNK * pair + CHUNK], jnp.concatenate(rights, 1))
            mixed += [both[:SIZE, :CHUNK], both[SIZE:, CHUNK:]]
        gated = by_head(jnp.concatenate(mixed, 0), growth, k) * silu_of_half(gates[:, span(k)])
        rounded.append(gated.astype(BF16))
        scale = lax.rsqrt(jnp.mean(gated * gated, axis=0, keepdims=True) + EPSILON)
        scales.append(jnp.transpose(jnp.broadcast_to(scale, (CHUNK, CHUNK))))

    for k in range(chunks):
        change = dot(rounded[k], out_w_ref[layer], ((0,), (0,)))
        result = h[span(k)] + change * jnp.concatenate([scales[k]] * parts, 1)
        if interleaved:
            line, first_x = k // per_line, CHUNK * (k % per_line)
            size = tokens // (lines * gx)
            for i in range(CHUNK // size):
                x = size * (gx - 1 - (first_x // size + i))
                for part in range(parts):
                    target = pl.ds((lines * x + line) * parts + part, size, stride=lines * parts)
                    mixed_ref[target, :] = result[size * i : size * i + size, span(part)]
        else:
            result = result.astype(BF16)
            size = tokens // gy
            for b in range(CHUNK // size):
                first = tokens - size * (k * (CHUNK // size) + b + 1)
                o_ref[first : first + size, :] = result[size * b : size * b + size]
    if interleaved:
        o_ref[...] = mixed_ref[...].astype(BF16)


def mix(x, layer, lines, grid, shape, weights):
    return pl.pallas_call(
        functools.partial(layer_kernel, layer, lines, grid),
        out_shape=jax.ShapeDtypeStruct(shape, BF16),
        in_specs=[pl.BlockSpec(memory_space=pltpu.VMEM)] * 4,
        out_specs=pl.BlockSpec(memory_space=pltpu.VMEM),
        scratch_shapes=[pltpu.VMEM((x.size // 128, 128), F32)] * 2,
        compiler_params=pltpu.CompilerParams(vmem_limit_bytes=32 * 1024 * 1024),
        name=f"mix_layer_{layer}",
    )(x, *weights)


def on_device(gx, gy, field, *weights):
    nx, ny, width = field.shape
    lines = ny // gx
    tokens = nx * ny
    weights = prepare(*weights)
    falling_x = [list(reversed(range(gx)))]
    falling_y = [list(reversed(range(gy)))]
    sent = spread(field).reshape(gx, lines * nx, width)
    taken = lax.all_to_all(sent, "gx", 0, 0, tiled=True, axis_index_groups=falling_x)
    taken = taken.reshape(tokens, width)
    stream = mix(taken, 0, lines, (gx, gy), (2 * tokens, width // 2), weights)
    owners = [list(reversed(range(gx * gy)))]
    taken = lax.all_to_all(
        stream.reshape(gx * nx, -1, width // 2),
        ("gx", "gy"),
        0,
        0,
        tiled=True,
        axis_index_groups=owners,
    )
    stream = mix(taken.reshape(stream.shape), 1, 1, (gx, gy), (tokens, width), weights)
    return lax.all_to_all(
        stream.reshape(gy, ny, width), "gy", 0, 0, tiled=True, axis_index_groups=falling_y
    )


def solution(mesh):
    in_specs = (P("gx", "gy", None), P(), P(), P(), P(), P(), P(), P(), P())
    return jax.shard_map(
        functools.partial(on_device, mesh.shape["gx"], mesh.shape["gy"]),
        mesh=mesh,
        in_specs=in_specs,
        out_specs=P("gx", "gy", None),
        check_vma=False,
    )
```

```python
import functools

import jax
import jax.numpy as jnp
from jax import lax
from jax.experimental import pallas as pl
from jax.experimental.pallas import tpu as pltpu
from jax.sharding import PartitionSpec as P

EPSILON = 1e-05
LOG2E = 1.4426950408889634
CHUNK = 128
HEADS = 8
SIZE = 64
ORDER = 64
INNER = HEADS * SIZE
F32 = jnp.float32
BF16 = jnp.bfloat16


def positions(rows, cols):
    return (
        lax.broadcasted_iota(jnp.int32, (rows, cols), 0),
        lax.broadcasted_iota(jnp.int32, (rows, cols), 1),
    )


def sum_matrix():
    s, t = positions(CHUNK, CHUNK)
    below = jnp.where(s < t, 1.0, jnp.where(s == t, 0.5, 0.0))
    return jnp.concatenate([below, jnp.ones((CHUNK, CHUNK), F32)], 1).astype(BF16)


def dot(a, b, dims=((1,), (0,))):
    return lax.dot_general(a, b, (dims, ((), ())), preferred_element_type=F32)


def silu_of_half(v):
    return v + v * jnp.tanh(v)


def backwards(v):
    return jnp.concatenate([v[i : i + 1] for i in reversed(range(v.shape[0]))], 0)


def rows16(row, rows):
    piece = jnp.broadcast_to(row, (16, row.shape[1])).astype(BF16)
    return jnp.concatenate([piece] * (rows // 16), 0)


def column(row):
    n = row.shape[1]
    square = lax.broadcasted_iota(jnp.int32, (n, n), 0) == lax.broadcasted_iota(
        jnp.int32, (n, n), 1
    )
    return jnp.sum(jnp.where(square, jnp.broadcast_to(row, (n, n)), 0.0), 1, keepdims=True)


def spread_kernel(field_ref, o_ref, taken, mixed, staged, in_sems, out_sems):
    nx, ny, width = field_ref.shape
    groups = in_sems.shape[0]
    size = ny // groups
    arriving = []
    for g in range(groups):
        part = pl.ds(size * g, size)
        arriving.append(
            pltpu.make_async_copy(field_ref.at[:, part, :], taken.at[:, part, :], in_sems.at[g])
        )
        arriving[-1].start()
    leaving = []
    for g in range(groups):
        arriving[g].wait()
        rows = slice(nx * size * g, nx * size * (g + 1))
        for half in range(width // 128):
            lanes = slice(128 * half, 128 * half + 128)
            first = nx * ny * half
            for x in range(nx):
                plane = taken[x, size * g : size * g + size, lanes].astype(F32)
                mixed[pl.ds(first + nx * size * g + x, size, stride=nx), :] = plane
            staged[rows, lanes] = mixed[first + rows.start : first + rows.stop, :].astype(BF16)
        part = pl.ds(nx * size * g, nx * size)
        leaving.append(pltpu.make_async_copy(staged.at[part], o_ref.at[part], out_sems.at[g]))
        leaving[-1].start()
    for copy in leaving:
        copy.wait()


def spread(field):
    nx, ny, width = field.shape
    groups = 4
    return pl.pallas_call(
        spread_kernel,
        out_shape=jax.ShapeDtypeStruct((ny * nx, width), BF16),
        in_specs=[pl.BlockSpec(memory_space=pl.ANY)],
        out_specs=pl.BlockSpec(memory_space=pl.ANY),
        scratch_shapes=[
            pltpu.VMEM(field.shape, BF16),
            pltpu.VMEM((ny * nx * width // 128, 128), F32),
            pltpu.VMEM((ny * nx, width), BF16),
            pltpu.SemaphoreType.DMA((groups,)),
            pltpu.SemaphoreType.DMA((groups,)),
        ],
        compiler_params=pltpu.CompilerParams(vmem_limit_bytes=62 * 1024 * 1024),
        name="spread_field",
    )(field)


def prepare_kernel(
    norm_ref,
    inner_ref,
    state_ref,
    step_ref,
    bias_ref,
    rate_ref,
    gain_ref,
    out_w_ref,
    weights_ref,
    out_ref,
    small_ref,
):
    base = 2 * HEADS + 2 * ORDER
    for layer in range(2):
        weights_ref[layer, : 2 * HEADS, :] = jnp.concatenate(
            [step_ref[layer], jnp.zeros_like(step_ref[layer])], 0
        )
        weights_ref[layer, 2 * HEADS : base, :] = jnp.transpose(state_ref[layer])
        inner = jnp.transpose(inner_ref[layer] * 0.5)
        weights_ref[layer, base : base + INNER, :] = inner[INNER:]
        weights_ref[layer, base + INNER :, :] = inner[:INNER]
        row = slice(layer, layer + 1)
        gain = jnp.transpose(jnp.broadcast_to(gain_ref[row, :], (CHUNK, INNER)))
        out_ref[layer] = (
            out_w_ref[layer].astype(F32) * jnp.concatenate([gain, gain], 1)
        ).astype(BF16)
        wide = (HEADS, INNER)
        small_ref[layer, :HEADS, :] = jnp.broadcast_to(column(bias_ref[row, :]), wide)
        small_ref[layer, HEADS : 2 * HEADS, :] = jnp.broadcast_to(column(rate_ref[row, :]), wide)
        norm = norm_ref[row, :]
        small_ref[layer, 2 * HEADS :, :] = jnp.broadcast_to(
            jnp.concatenate([norm, norm], 1), wide
        )


def prepare(norm_gain, inner, state, step, bias, rate, gain, out_weight):
    step = jnp.swapaxes(step, 1, 2)
    rows = inner.shape[2] + state.shape[2] + 2 * HEADS
    return pl.pallas_call(
        prepare_kernel,
        out_shape=(
            jax.ShapeDtypeStruct((2, rows, inner.shape[1]), BF16),
            jax.ShapeDtypeStruct(out_weight.shape, BF16),
            jax.ShapeDtypeStruct((2, 3 * HEADS, INNER), F32),
        ),
        in_specs=[pl.BlockSpec(memory_space=pltpu.VMEM)] * 8,
        out_specs=[pl.BlockSpec(memory_space=pltpu.VMEM)] * 3,
        compiler_params=pltpu.CompilerParams(vmem_limit_bytes=16 * 1024 * 1024),
        cost_estimate=pl.CostEstimate(flops=0, bytes_accessed=4 * 1024 * 1024, transcendentals=0),
        name="prepare_weights",
    )(norm_gain, inner, state, step, bias, rate, gain, out_weight)


def layer_kernel(
    layer, lines, grid, x_ref, weights_ref, out_w_ref, small_ref, o_ref, mixed_ref, sorted_ref
):
    interleaved = lines > 1
    width = weights_ref.shape[2]
    parts = width // 128
    tokens = x_ref.size // width
    chunks = tokens // CHUNK
    per_line = chunks // lines
    gx, gy = grid
    h = x_ref[...].astype(F32)
    if not interleaved:
        pair = tokens // (gx * gy)
        mixed_ref[...] = h
        for part in range(parts):
            for l in range(pair):
                found = mixed_ref[pl.ds(l * parts + part, gx * gy, stride=pair * parts), :]
                found = jnp.swapaxes(found.reshape(gx, gy, 128), 0, 1)
                found = backwards(found).reshape(gx * gy, 128)
                sorted_ref[pl.ds(part * tokens + l, gx * gy, stride=pair), :] = found
        h = jnp.concatenate(
            [sorted_ref[part * tokens : part * tokens + tokens, :] for part in range(parts)], 1
        )
    else:
        h = jnp.concatenate(
            [
                h[8 * (lines * g + l) : 8 * (lines * g + l) + 8]
                for l in range(lines)
                for g in reversed(range(tokens // (8 * lines)))
            ],
            0,
        )
    scale = lax.rsqrt(jnp.mean(h * h, axis=1, keepdims=True) + EPSILON)
    normed = (h * scale * small_ref[layer, 2 * HEADS : 2 * HEADS + 1, : h.shape[1]]).astype(BF16)

    rows = weights_ref.shape[1] - INNER
    projected = dot(weights_ref[layer, :rows, :], normed, ((1,), (1,)))
    raw_steps = projected[:HEADS]
    base = 2 * HEADS
    enter = projected[base : base + ORDER].astype(BF16)
    leave = projected[base + ORDER : base + 2 * ORDER].astype(BF16)
    base += 2 * ORDER
    inputs = silu_of_half(projected[base : base + INNER]).astype(BF16)
    raw_steps = raw_steps + small_ref[layer, :HEADS, :]
    steps = jnp.maximum(raw_steps, 0.0) + jnp.log1p(jnp.exp(-jnp.abs(raw_steps)))
    decay = -steps * small_ref[layer, HEADS : 2 * HEADS, :]
    steps = jnp.concatenate([steps[:, CHUNK * k : CHUNK * k + CHUNK] for k in range(chunks)], 0)
    decay = jnp.concatenate([decay[:, CHUNK * k : CHUNK * k + CHUNK] for k in range(chunks)], 0)
    first = decay.astype(BF16)
    rest = decay - first.astype(F32)
    second = rest.astype(BF16)
    third = (rest - second.astype(F32)).astype(BF16)
    summed = dot(jnp.concatenate([first, second, third], 0), sum_matrix())
    gates = dot(weights_ref[layer, rows:, :], normed, ((1,), (1,)))
    n = HEADS * chunks
    summed = summed[:n] + summed[n : 2 * n] + summed[2 * n :]
    mid = summed[:, :CHUNK]
    whole = summed[:, CHUNK:]
    lead = jnp.exp(mid)
    tail = jnp.exp(whole - mid)
    entry = steps * jnp.exp(-0.5 * decay)
    entry_tail = entry * tail
    entry_lead = entry * lead
    growth = jnp.exp(0.5 * decay)
    total = jnp.exp(whole)
    mid2 = mid * LOG2E
    mid2_columns = jnp.transpose(
        jnp.concatenate([mid2, jnp.zeros((CHUNK - n, CHUNK), F32)], 0)
    )

    s_pos, t_pos = positions(CHUNK, CHUNK)
    double = jnp.where(s_pos == t_pos, 2.0, 1.0)
    falling = jnp.where(s_pos < t_pos, -1.0, 1.0).astype(BF16)
    ahead_half = t_pos < ORDER

    def span(k):
        return slice(CHUNK * k, CHUNK * k + CHUNK)

    def by_head(values, rows, k):
        return jnp.concatenate(
            [
                values[SIZE * h : SIZE * h + SIZE] * rows[HEADS * k + h : HEADS * k + h + 1]
                for h in range(HEADS)
            ],
            0,
        )

    entered = []
    carried_ahead = []
    carried_behind = []
    for k in range(chunks):
        x = inputs[:, span(k)]
        for kept, factors in (
            (entered, entry),
            (carried_ahead, entry_tail),
            (carried_behind, entry_lead),
        ):
            kept.append(
                jnp.concatenate(
                    [
                        x[SIZE * h : SIZE * h + SIZE]
                        * rows16(factors[HEADS * k + h : HEADS * k + h + 1], SIZE)
                        for h in range(HEADS)
                    ],
                    0,
                )
            )

    empty = jnp.zeros((ORDER, CHUNK), BF16)
    joined = [None] * chunks
    for line in range(lines):
        start = line * per_line
        states = [jnp.zeros((INNER, CHUNK), F32)]
        for j in range(per_line - 1):
            f, b = start + j, start + per_line - 1 - j
            sides = jnp.concatenate(
                [
                    jnp.concatenate([enter[:, span(f)], empty], 1),
                    jnp.concatenate([empty, enter[:, span(b)]], 1),
                ],
                0,
            )
            end = dot(
                jnp.concatenate([carried_ahead[f], carried_behind[b]], 1), sides, ((1,), (1,))
            )
            factor = jnp.where(
                ahead_half[:HEADS],
                total[HEADS * f : HEADS * f + HEADS],
                total[HEADS * b : HEADS * b + HEADS],
            )
            states.append(by_head(states[-1], factor, 0) + end)
        for j in range(per_line):
            mirror = states[per_line - 1 - j]
            ahead = jnp.concatenate([ahead_half] * (INNER // CHUNK), 0)
            joined[start + j] = jnp.where(ahead, states[j], mirror).astype(BF16)

    rounded = []
    scales = []
    for k in range(chunks):
        left = jnp.concatenate([entered[k], joined[k]], 1)
        leave_k = leave[:, span(k)]
        scores = (dot(enter[:, span(k)], leave_k, ((0,), (0,))) * double).astype(BF16)
        mixed = []
        for pair in range(HEADS // 2):
            rights = []
            for row in (HEADS * k + 2 * pair, HEADS * k + 2 * pair + 1):
                gap = mid2_columns[:, row : row + 1] - mid2[row : row + 1]
                mixing = scores * jnp.exp2(gap.astype(BF16) * falling)
                rights.append(
                    jnp.concatenate(
                        [
                            mixing,
                            leave_k * rows16(lead[row : row + 1], ORDER),
                            leave_k * rows16(tail[row : row + 1], ORDER),
                        ],
                        0,
                    )
                )
            both = dot(left[CHUNK * pair : CHUNK * pair + CHUNK], jnp.concatenate(rights, 1))
            mixed += [both[:SIZE, :CHUNK], both[SIZE:, CHUNK:]]
        gated = by_head(jnp.concatenate(mixed, 0), growth, k) * silu_of_half(gates[:, span(k)])
        rounded.append(gated.astype(BF16))
        scale = lax.rsqrt(jnp.mean(gated * gated, axis=0, keepdims=True) + EPSILON)
        scales.append(jnp.transpose(jnp.broadcast_to(scale, (CHUNK, CHUNK))))

    for k in range(chunks):
        change = dot(rounded[k], out_w_ref[layer], ((0,), (0,)))
        result = h[span(k)] + change * jnp.concatenate([scales[k]] * parts, 1)
        if interleaved:
            line, first_x = k // per_line, CHUNK * (k % per_line)
            size = tokens // (lines * gx)
            for i in range(CHUNK // size):
                x = size * (gx - 1 - (first_x // size + i))
                for part in range(parts):
                    target = pl.ds((lines * x + line) * parts + part, size, stride=lines * parts)
                    mixed_ref[target, :] = result[size * i : size * i + size, span(part)]
        else:
            result = result.astype(BF16)
            size = tokens // gy
            for b in range(CHUNK // size):
                first = tokens - size * (k * (CHUNK // size) + b + 1)
                o_ref[first : first + size, :] = result[size * b : size * b + size]
    if interleaved:
        o_ref[...] = mixed_ref[...].astype(BF16)


def mix(x, layer, lines, grid, shape, weights):
    return pl.pallas_call(
        functools.partial(layer_kernel, layer, lines, grid),
        out_shape=jax.ShapeDtypeStruct(shape, BF16),
        in_specs=[pl.BlockSpec(memory_space=pltpu.VMEM)] * 4,
        out_specs=pl.BlockSpec(memory_space=pltpu.VMEM),
        scratch_shapes=[pltpu.VMEM((x.size // 128, 128), F32)] * 2,
        compiler_params=pltpu.CompilerParams(vmem_limit_bytes=32 * 1024 * 1024),
        name=f"mix_layer_{layer}",
    )(x, *weights)


def on_device(gx, gy, field, *weights):
    nx, ny, width = field.shape
    lines = ny // gx
    tokens = nx * ny
    weights = prepare(*weights)
    falling_x = [list(reversed(range(gx)))]
    falling_y = [list(reversed(range(gy)))]
    sent = spread(field).reshape(gx, lines * nx, width)
    taken = lax.all_to_all(sent, "gx", 0, 0, tiled=True, axis_index_groups=falling_x)
    taken = taken.reshape(tokens, width)
    stream = mix(taken, 0, lines, (gx, gy), (2 * tokens, width // 2), weights)
    owners = [list(reversed(range(gx * gy)))]
    taken = lax.all_to_all(
        stream.reshape(gx * nx, -1, width // 2),
        ("gx", "gy"),
        0,
        0,
        tiled=True,
        axis_index_groups=owners,
    )
    stream = mix(taken.reshape(stream.shape), 1, 1, (gx, gy), (tokens, width), weights)
    return lax.all_to_all(
        stream.reshape(gy, ny, width), "gy", 0, 0, tiled=True, axis_index_groups=falling_y
    )


def solution(mesh):
    in_specs = (P("gx", "gy", None), P(), P(), P(), P(), P(), P(), P(), P())
    return jax.shard_map(
        functools.partial(on_device, mesh.shape["gx"], mesh.shape["gy"]),
        mesh=mesh,
        in_specs=in_specs,
        out_specs=P("gx", "gy", None),
        check_vma=False,
    )
```
